32 devices in a mesh: rep: 4 (over z), blk: 8 (over y, x, core).
Axes of the slice: x: 2, y: 2, z: 4, core: 2. Of those that a mesh axis runs over, the one named last changes fastest.
Arguments:
- feats: bfloat16 [4096, 256], P(('blk', 'rep')), may hold values from -6 to 6
- weight: bfloat16 [256, 256], replicated, may hold values from -0.375 to 0.375
- cotangent: bfloat16 [4096, 256], P(('blk', 'rep')), may hold values from -6 to 6
- block_vals: bfloat16 [8, 4, 2, 3, 128, 128], P('blk', 'rep'), may hold values from -0.109375 to 0.109375
- block_rows: int32 [8, 4, 2, 3], P('blk', 'rep'), may hold values from 0 to 3
- block_cols: int32 [8, 4, 2, 3], P('blk', 'rep'), may hold values from 0 to 3
- step_counts: int32 [8, 4, 2], P('blk', 'rep'), may hold values from 0 to 3, as said below
Outputs:
- out_rows: bfloat16 [4096, 256], P(('blk', 'rep'))
- grad_weight: float32 [256, 256], replicated
- grad_feats: float32 [4096, 256], P(('blk', 'rep'))
The draws below stay inside these ranges and needn't reach their ends.
Inputs may be any that keep to these rules, and one draw needn't show every extreme that they name: `step_counts`: every list (g, m) reaches 3 live slots at one or more of its j.
All inputs are finite; a program needn't handle non-finite values.
Results may differ from the reference program's by a relative error of at most 0.0055.
Values may be sent and summed in bfloat16 or wider, within the bound.
No kernel may reach another device: no remote copies, remote signals or barrier semaphores. Data moves between devices by JAX's collectives and lax.ppermute only.
A program may use at most 64 MiB of HBM per device.

```python
import jax
import jax.numpy as jnp
from jax import lax

F = 256
BLOCK = 128
CAP = 3
STEPS = 2
RB = 4
NBR = 32
N_NODES = 4096
N_REP = 4
N_BLK = 8


def draw_step_counts(key, part):
    key = jax.random.fold_in(key, 5)
    base_key, forced_key = jax.random.split(key)
    base = jax.random.randint(base_key, (N_BLK, N_REP, STEPS), 0, CAP + 1)
    forced = jax.random.randint(forced_key, (N_BLK, N_REP, 1), 0, STEPS)
    step_ids = jnp.arange(STEPS, dtype=jnp.int32)[None, None, :]
    return jnp.where(step_ids == forced, CAP, base).astype(jnp.int32)


def touch_ends(values, own_key, least, largest):
    dims = values.shape
    index_at = [jax.random.randint(jax.random.fold_in(own_key, axis), (), 0, dims[axis]) for axis in range(len(dims))]
    values = values.at[tuple(index_at)].set(least)
    longest = dims.index(max(dims))
    index_at[longest] = (index_at[longest] + 1) % dims[longest]
    return values.at[tuple(index_at)].set(largest)


def level_of(rng, dims, shards, least, top_value):
    level = 1.0
    for position, parts in shards:
        heights = jax.random.uniform(jax.random.fold_in(jax.random.fold_in(rng, 6), position), (parts,), jnp.float32, least / len(shards), top_value / len(shards))
        level = level * jnp.repeat(jnp.exp(heights), dims[position] // parts).reshape((-1,) + (1,) * (len(dims) - 1 - position))
    return level


def scatter_about(own_key, dims, scale, limit, pieces=(), kind=jnp.bfloat16):
    gain = level_of(own_key, dims, pieces, -0.22, 0.18) if pieces else 1.0
    values = jax.random.normal(own_key, dims, jnp.float32) * scale * gain
    return jnp.minimum(jnp.maximum(values, -limit), limit).astype(kind)


def setup_inputs(seed: int = 0) -> dict:
    keys = jax.random.split(jax.random.key(seed), 8)
    feats = scatter_about(keys[0], (N_NODES, F), 1.0, 6.0, ((0, 32),))
    weight = scatter_about(keys[1], (F, F), F ** -0.5, 0.375)
    cotangent = scatter_about(keys[2], (N_NODES, F), 1.0, 6.0, ((0, 32),))
    block_vals = scatter_about(keys[3], (N_BLK, N_REP, STEPS, CAP, BLOCK, BLOCK), (24 * BLOCK) ** -0.5, 0.109375, ((0, 8), (1, 4)))
    block_rows = touch_ends(jax.random.randint(keys[4], (N_BLK, N_REP, STEPS, CAP), 0, RB), jax.random.fold_in(keys[4], 1), 0, RB - 1).astype(jnp.int32)
    block_cols = touch_ends(jax.random.randint(keys[5], (N_BLK, N_REP, STEPS, CAP), 0, RB), jax.random.fold_in(keys[5], 1), 0, RB - 1).astype(jnp.int32)
    step_counts = draw_step_counts(jax.random.fold_in(keys[7], 71), 0)
    return {"feats": feats, "weight": weight, "cotangent": cotangent, "block_vals": block_vals, "block_rows": block_rows, "block_cols": block_cols, "step_counts": step_counts}


def silu_parts(pre):
    sigma = jax.nn.sigmoid(pre)
    return pre * sigma, sigma * (1.0 + pre * (1.0 - sigma))


def block_indices(block_rows, block_cols, step_counts):
    cycle_pos = jnp.arange(N_BLK, dtype=jnp.int32)[:, None, None, None]
    member = jnp.arange(N_REP, dtype=jnp.int32)[None, :, None, None]
    offset = jnp.arange(STEPS, dtype=jnp.int32)[None, None, :, None]
    row_block = cycle_pos * RB + block_rows
    col_block = ((cycle_pos - member * STEPS - offset) % N_BLK) * RB + block_cols
    slot_ids = jnp.arange(CAP, dtype=jnp.int32)[None, None, None, :]
    live_mask = slot_ids < step_counts[:, :, :, None]
    return row_block.astype(jnp.int32), col_block.astype(jnp.int32), live_mask


def reference(feats, weight, cotangent, block_vals, block_rows, block_cols, step_counts):
    row_block, col_block, live_mask = block_indices(block_rows, block_cols, step_counts)
    feat_blocks = feats.reshape(NBR, BLOCK, F)

    def forward_scan(carry, items):
        adjacency, rows_now, cols_now, live_now = items
        adjacency = adjacency.reshape(-1, BLOCK, BLOCK).astype(jnp.float32)
        adjacency = adjacency * live_now.reshape(-1).astype(jnp.float32)[:, None, None]
        source = feat_blocks[cols_now.reshape(-1)].astype(jnp.float32)
        products = jnp.einsum("kij,kjf->kif", adjacency, source)
        return carry.at[rows_now.reshape(-1)].add(products), None

    start = jnp.zeros((NBR, BLOCK, F), jnp.float32)
    aggregate, unused = lax.scan(forward_scan, start, (block_vals, row_block, col_block, live_mask))
    aggregate = aggregate.reshape(N_NODES, F).astype(jnp.bfloat16)
    pre = jnp.dot(aggregate, weight, preferred_element_type=jnp.float32)
    activated, slope = silu_parts(pre)
    out_rows = activated.astype(jnp.bfloat16)
    dpre = (cotangent.astype(jnp.float32) * slope).astype(jnp.bfloat16)
    grad_weight = jnp.dot(aggregate.T, dpre, preferred_element_type=jnp.float32)
    dagg = jnp.dot(dpre, weight.T, preferred_element_type=jnp.float32).astype(jnp.bfloat16)
    grad_blocks = dagg.reshape(NBR, BLOCK, F)

    def backward_scan(carry, items):
        adjacency, rows_now, cols_now, live_now = items
        adjacency = adjacency.reshape(-1, BLOCK, BLOCK).astype(jnp.float32)
        adjacency = adjacency * live_now.reshape(-1).astype(jnp.float32)[:, None, None]
        source = grad_blocks[rows_now.reshape(-1)].astype(jnp.float32)
        products = jnp.einsum("kji,kjf->kif", adjacency, source)
        return carry.at[cols_now.reshape(-1)].add(products), None

    grad_feats, unused = lax.scan(backward_scan, start, (block_vals, row_block, col_block, live_mask))
    return out_rows, grad_weight, grad_feats.reshape(N_NODES, F)
```

```python
import functools

import jax
import jax.numpy as jnp
from jax import lax
from jax.experimental import pallas as pl
from jax.experimental.pallas import tpu as pltpu
from jax.sharding import PartitionSpec as P

F32 = jnp.float32
BF16 = jnp.bfloat16
VMEM = pl.BlockSpec(memory_space=pltpu.VMEM)
SMEM = pl.BlockSpec(memory_space=pltpu.SMEM)


def shift(array, axis, by):
    peers = lax.axis_size(axis)
    return lax.ppermute(array, axis, [(i, (i + by) % peers) for i in range(peers)])


def call(body, outs, in_specs, scratch=(), flops=0, moved=0):
    return pl.pallas_call(
        body,
        out_shape=outs,
        in_specs=in_specs,
        out_specs=jax.tree.map(lambda _: VMEM, outs),
        scratch_shapes=list(scratch),
        compiler_params=pltpu.CompilerParams(vmem_limit_bytes=48 * 1024 * 1024),
        cost_estimate=pl.CostEstimate(flops=flops, bytes_accessed=moved, transcendentals=0),
    )


def member_and(by, reps):
    return lax.rem(lax.axis_index("rep") + by, reps)


def split_features(reps, width, feats, *rest):
    outs, turned = rest[:-1], rest[-1]
    turned[...] = feats[...].astype(F32).T.astype(BF16).reshape(turned.shape)
    for t in range(reps):
        outs[t][...] = turned[member_and(t, reps)]


def slot_of(index, lists, cap, j, c):
    k = j * cap + c
    row = index[k]
    col = index[lists * cap + k]
    live = c < index[2 * lists * cap + j]
    return row, col, live


def aggregate(reps, lists, cap, *refs):
    groups = reps * lists
    index = refs[:reps]
    blocks = refs[reps : 2 * reps]
    parts = refs[2 * reps : 2 * reps + groups]
    outs = refs[2 * reps + groups : 3 * reps + groups]
    held, total = refs[3 * reps + groups :]
    for s in range(groups):
        held[s] = parts[s][...]
    total[...] = jnp.zeros_like(total)
    for t in range(reps):
        origin = member_and(reps - t, reps)
        for j in range(lists):
            s = origin * lists + j
            for c in range(cap):
                row, col, live = slot_of(index[t], lists, cap, j, c)
                place = member_and(reps - col, reps)
                product = lax.dot_general(
                    held[s, place],
                    blocks[t][j * cap + c],
                    (((1,), (1,)), ((), ())),
                    preferred_element_type=F32,
                )
                total[row] += jnp.where(live, product, 0.0)
    for t in range(reps):
        outs[t][...] = total[member_and(t, reps)].astype(BF16)


def dense_layer(reps, *refs):
    chunks = refs[:reps]
    weight, cotangent, out, agg_out, dpre_out = refs[reps : reps + 5]
    dagg_outs = refs[reps + 5 : 2 * reps + 5]
    agg, dagg = refs[2 * reps + 5 :]
    for t in range(reps):
        agg[member_and(reps - t, reps)] = chunks[t][...]
    turned = agg[...].reshape(-1, agg.shape[2])
    agg_out[...] = turned
    pre = lax.dot_general(
        turned, weight[...], (((0,), (0,)), ((), ())), preferred_element_type=F32
    )
    sigma = jax.nn.sigmoid(pre)
    out[...] = (pre * sigma).astype(BF16)
    slope = sigma * (1.0 + pre * (1.0 - sigma))
    dpre = (cotangent[...].astype(F32) * slope).astype(BF16)
    dpre_out[...] = dpre
    dagg[...] = (
        lax.dot_general(
            weight[...], dpre, (((1,), (1,)), ((), ())), preferred_element_type=F32
        )
        .astype(BF16)
        .reshape(dagg.shape)
    )
    for t in range(reps):
        dagg_outs[t][...] = dagg[member_and(t, reps)]


def weight_terms(reps, agg, dpre, *rest):
    outs, terms = rest[:-1], rest[-1]
    product = jnp.dot(agg[...], dpre[...], preferred_element_type=F32)
    terms[...] = product.astype(BF16).reshape(terms.shape)
    for t in range(reps):
        outs[t][...] = terms[member_and(t, reps)]


def feature_grads(reps, lists, cap, *refs):
    groups = reps * lists
    index = refs[:reps]
    blocks = refs[reps : 2 * reps]
    chunks = refs[2 * reps : 3 * reps]
    outs = refs[3 * reps : 3 * reps + groups]
    dagg, total = refs[3 * reps + groups :]
    for t in range(reps):
        dagg[member_and(reps - t, reps)] = chunks[t][...]
    total[...] = jnp.zeros_like(total)
    for t in range(reps):
        origin = member_and(reps - t, reps)
        for j in range(lists):
            s = origin * lists + j
            for c in range(cap):
                row, col, live = slot_of(index[t], lists, cap, j, c)
                product = jnp.dot(
                    dagg[row], blocks[t][j * cap + c], preferred_element_type=F32
                )
                total[s, col] += jnp.where(live, product, 0.0)
    for s in range(groups):
        outs[s][...] = total[s].astype(BF16)


def sum_all(*refs):
    out = refs[-1]
    total = refs[0][...].astype(F32)
    for ref in refs[1:-1]:
        total += ref[...].astype(F32)
    out[...] = total.astype(out.dtype)


def sum_groups(reps, groups, *refs):
    parts = refs[:groups]
    outs = refs[groups : groups + reps]
    for t in range(reps):
        place = member_and(t, reps)
        total = parts[0][place].astype(F32)
        for part in parts[1:]:
            total += part[place].astype(F32)
        outs[t][...] = total.astype(BF16)


def join_rows(reps, *refs):
    chunks, out, joined = refs[:reps], refs[reps], refs[reps + 1]
    for t in range(reps):
        joined[member_and(reps - t, reps)] = chunks[t][...].astype(F32)
    out[...] = joined[...].reshape(-1, joined.shape[2]).T


def join_weight(reps, *refs):
    chunks, out = refs[:reps], refs[reps]
    part = out.shape[0] // reps
    for t in range(reps):
        start = pl.multiple_of(member_and(reps - t, reps) * part, part)
        out[pl.ds(start, part), :] = chunks[t][...].astype(F32)


def per_device(feats, weight, cotangent, block_vals, block_rows, block_cols, step_counts):
    reps = lax.axis_size("rep")
    groups = lax.axis_size("blk")
    lists, cap, block = block_vals.shape[2:5]
    nodes, width = feats.shape
    part = width // reps
    like = jax.ShapeDtypeStruct
    chunk = like((part, block), BF16)
    wchunk = like((part, width), BF16)
    group = like((reps, part, block), BF16)

    def over_rep(arrays):
        return [arrays[0]] + [shift(arrays[t], "rep", t) for t in range(1, reps)]

    index = jnp.concatenate(
        [block_rows.reshape(-1), block_cols.reshape(-1), step_counts.reshape(-1)]
    )
    blocks = block_vals.reshape(lists * cap, block, block)

    quarters = call(
        functools.partial(split_features, reps, width),
        [chunk] * reps,
        [VMEM],
        [pltpu.VMEM((reps, part, block), BF16)],
        moved=2 * nodes * width * 2,
    )(feats)
    quarters = over_rep(quarters)
    all_index = over_rep([index] * reps)
    all_blocks = over_rep([blocks] * reps)
    mine = jnp.stack(quarters)
    feats_parts = [mine] + [shift(mine, "blk", s) for s in range(1, groups)]
    slots = groups * cap
    slot_flops = 2 * slots * part * block * block
    slot_bytes = 2 * (slots * block * block + groups * reps * part * block)

    chunks = call(
        functools.partial(aggregate, reps, lists, cap),
        [chunk] * reps,
        [SMEM] * reps + [VMEM] * (reps + groups),
        [
            pltpu.VMEM((groups, reps, part, block), BF16),
            pltpu.VMEM((reps, part, block), F32),
        ],
        flops=slot_flops,
        moved=slot_bytes,
    )(*all_index, *all_blocks, *feats_parts)
    chunks = over_rep(chunks)

    out_rows, agg, dpre, *dagg = call(
        functools.partial(dense_layer, reps),
        [
            like((nodes, width), BF16),
            like((width, nodes), BF16),
            like((nodes, width), BF16),
        ]
        + [chunk] * reps,
        [VMEM] * (reps + 2),
        [pltpu.VMEM((reps, part, block), BF16)] * 2,
        flops=4 * nodes * width * width,
        moved=14 * nodes * width,
    )(*chunks, weight, cotangent)
    dagg = over_rep(dagg)

    terms = call(
        functools.partial(weight_terms, reps),
        [wchunk] * reps,
        [VMEM] * 2,
        [pltpu.VMEM((reps, part, width), BF16)],
        flops=2 * nodes * width * width,
        moved=8 * nodes * width,
    )(agg, dpre)
    terms = over_rep(terms)

    grads = call(
        functools.partial(feature_grads, reps, lists, cap),
        [group] * groups,
        [SMEM] * reps + [VMEM] * (2 * reps),
        [
            pltpu.VMEM((reps, part, block), BF16),
            pltpu.VMEM((groups, reps, part, block), F32),
        ],
        flops=slot_flops,
        moved=slot_bytes,
    )(*all_index, *all_blocks, *dagg)
    grads = [grads[0]] + [shift(grads[s], "blk", -s) for s in range(1, groups)]

    term = call(sum_all, wchunk, [VMEM] * reps, moved=5 * 2 * part * width)(*terms)
    group_terms = [term] + [shift(term, "blk", s) for s in range(1, groups)]

    rows = call(
        functools.partial(sum_groups, reps, groups),
        [chunk] * reps,
        [VMEM] * groups,
        moved=2 * groups * reps * part * block,
    )(*grads)
    rows = over_rep(rows)

    gw_part = call(sum_all, wchunk, [VMEM] * groups, moved=2 * groups * part * width)(*group_terms)
    gw_parts = over_rep([gw_part] * reps)

    grad_feats = call(
        functools.partial(join_rows, reps),
        like((nodes, width), F32),
        [VMEM] * reps,
        [pltpu.VMEM((reps, part, block), F32)],
        moved=6 * nodes * width,
    )(*rows)
    grad_weight = call(
        functools.partial(join_weight, reps),
        like((width, width), F32),
        [VMEM] * reps,
        moved=6 * width * width,
    )(*gw_parts)
    return (out_rows, grad_weight, grad_feats)


def solution(mesh):
    return jax.shard_map(
        per_device,
        mesh=mesh,
        in_specs=(
            P(("blk", "rep"), None),
            P(),
            P(("blk", "rep"), None),
            P("blk", "rep", None, None, None, None),
            P("blk", "rep", None, None),
            P("blk", "rep", None, None),
            P("blk", "rep", None),
        ),
        out_specs=(P(("blk", "rep"), None), P(), P(("blk", "rep"), None)),
        check_vma=False,
    )
```

```python
import functools

import jax
import jax.numpy as jnp
from jax import lax
from jax.experimental import pallas as pl
from jax.experimental.pallas import tpu as pltpu
from jax.sharding import PartitionSpec as P

F32 = jnp.float32
BF16 = jnp.bfloat16
VMEM = pl.BlockSpec(memory_space=pltpu.VMEM)
SMEM = pl.BlockSpec(memory_space=pltpu.SMEM)
PAD = 16


def shift(array, axis, by):
    peers = lax.axis_size(axis)
    return lax.ppermute(array, axis, [(i, (i + by) % peers) for i in range(peers)])


def exchange(array, axis):
    return lax.all_to_all(array, axis, 0, 0, tiled=True)


def call(body, outs, in_specs, scratch=(), flops=0, moved=0):
    return pl.pallas_call(
        body,
        out_shape=outs,
        in_specs=in_specs,
        out_specs=jax.tree.map(lambda _: VMEM, outs),
        scratch_shapes=list(scratch),
        compiler_params=pltpu.CompilerParams(vmem_limit_bytes=48 * 1024 * 1024),
        cost_estimate=pl.CostEstimate(flops=flops, bytes_accessed=moved, transcendentals=0),
    )


def split_features(reps, lists, cap, feats, rows, cols, counts, out):
    nodes = feats.shape[0]
    part = feats.shape[1] // reps
    turned = feats[...].astype(F32).T.astype(BF16)
    lane = lax.broadcasted_iota(jnp.int32, (PAD, nodes), 1)
    index = jnp.zeros((PAD, nodes), jnp.int32)
    slots = lists * cap
    for j in range(lists):
        for c in range(cap):
            k = j * cap + c
            index = jnp.where(lane == k, rows[j, c], index)
            index = jnp.where(lane == slots + k, cols[j, c], index)
        index = jnp.where(lane == 2 * slots + j, counts[j], index)
    index = index.astype(F32).astype(BF16)
    for q in range(reps):
        out[q, :part] = turned[q * part : (q + 1) * part]
        out[q, part:] = index


def spread(groups, part, mine, out):
    own = mine[:, :part]
    for g in range(groups):
        out[g] = own


def slot_of(index, lists, cap, t, j, c):
    k = j * cap + c
    slots = lists * cap
    return index[t, k], index[t, slots + k], c < index[t, 2 * slots + j]


def aggregate(reps, groups, lists, cap, index, *refs):
    blocks = refs[:reps]
    held, out, total = refs[reps:]
    me = lax.axis_index("rep")
    mine = lax.axis_index("blk")
    total[...] = jnp.zeros_like(total)
    for t in range(reps):
        origin = lax.rem(me + reps - t, reps)
        for j in range(lists):
            source = lax.rem(mine + groups - origin * lists - j, groups)
            for c in range(cap):
                row, col, live = slot_of(index, lists, cap, origin, j, c)
                product = lax.dot_general(
                    held[source, col],
                    blocks[t][j * cap + c],
                    (((1,), (1,)), ((), ())),
                    preferred_element_type=F32,
                )
                total[row] += jnp.where(live, product, 0.0)
    out[...] = total[...].astype(BF16)


def dense_layer(reps, agg, weight, cotangent, out, send):
    part = agg.shape[1]
    nodes = agg.shape[2]
    turned = agg[...].reshape(reps * part, nodes)
    pre = lax.dot_general(
        turned, weight[...], (((0,), (0,)), ((), ())), preferred_element_type=F32
    )
    sigma = jax.nn.sigmoid(pre)
    out[...] = (pre * sigma).astype(BF16)
    slope = sigma * (1.0 + pre * (1.0 - sigma))
    dpre = (cotangent[...].astype(F32) * slope).astype(BF16)
    dagg = lax.dot_general(
        weight[...], dpre, (((1,), (1,)), ((), ())), preferred_element_type=F32
    )
    send[:, :, :nodes] = dagg.astype(BF16).reshape(reps, part, nodes)
    terms = jnp.dot(turned, dpre, preferred_element_type=F32)
    send[:, :, nodes:] = terms.astype(BF16).reshape(reps, part, reps * part)


def feature_grads(reps, groups, lists, cap, index, *refs):
    blocks = refs[:reps]
    arrived, out, total = refs[reps:]
    nodes = blocks[0].shape[1]
    me = lax.axis_index("rep")
    mine = lax.axis_index("blk")
    total[...] = jnp.zeros_like(total)
    for t in range(reps):
        origin = lax.rem(me + reps - t, reps)
        for j in range(lists):
            target = lax.rem(mine + groups - origin * lists - j, groups)
            for c in range(cap):
                row, col, live = slot_of(index, lists, cap, origin, j, c)
                product = jnp.dot(
                    arrived[row, :, :nodes], blocks[t][j * cap + c], preferred_element_type=F32
                )
                total[target, col] += jnp.where(live, product, 0.0)
    terms = arrived[0, :, nodes:].astype(F32)
    for t in range(1, reps):
        terms += arrived[t, :, nodes:].astype(F32)
    terms = terms.astype(BF16)
    for g in range(groups):
        for b in range(reps):
            out[g, :, b * nodes : (b + 1) * nodes] = total[g, b].astype(BF16)
        out[g, :, reps * nodes :] = terms


def sum_groups(reps, groups, arrived, out):
    nodes = (arrived.shape[2] - out.shape[2]) // (reps - 1)
    total = arrived[0].astype(F32)
    for g in range(1, groups):
        total += arrived[g].astype(F32)
    total = total.astype(BF16)
    for b in range(reps):
        out[b, :, :nodes] = total[:, b * nodes : (b + 1) * nodes]
        out[b, :, nodes:] = total[:, reps * nodes :]


def finish(reps, arrived, grad_feats, grad_weight):
    part = arrived.shape[1]
    nodes = grad_feats.shape[0]
    turned = arrived[:, :, :nodes].astype(F32).reshape(reps * part, nodes)
    grad_feats[...] = turned.T
    grad_weight[...] = arrived[:, :, nodes:].astype(F32).reshape(reps * part, -1)


def per_device(feats, weight, cotangent, block_vals, block_rows, block_cols, step_counts):
    reps = lax.axis_size("rep")
    groups = lax.axis_size("blk")
    lists, cap, block = block_vals.shape[2:5]
    nodes, width = feats.shape
    part = width // reps
    like = jax.ShapeDtypeStruct
    slots = lists * cap
    blocks = block_vals.reshape(slots, block, block)

    quarters = call(
        functools.partial(split_features, reps, lists, cap),
        like((reps, part + PAD, nodes), BF16),
        [VMEM, SMEM, SMEM, SMEM],
        moved=4 * nodes * width,
    )(feats, block_rows[0, 0], block_cols[0, 0], step_counts[0, 0])
    quarters = exchange(quarters, "rep")
    all_blocks = [blocks] + [shift(blocks, "rep", t) for t in range(1, reps)]
    index = quarters[:, part, : 2 * slots + lists].astype(jnp.int32)

    held = call(
        functools.partial(spread, groups, part),
        like((groups, reps, part, nodes), BF16),
        [VMEM],
        moved=2 * (groups + 1) * nodes * width,
    )(quarters)
    held = exchange(held, "blk")
    slot_flops = 2 * groups * cap * part * block * block
    slot_bytes = 2 * (groups * cap * block * block + groups * nodes * width)

    agg = call(
        functools.partial(aggregate, reps, groups, lists, cap),
        like((reps, part, nodes), BF16),
        [SMEM] + [VMEM] * (reps + 1),
        [pltpu.VMEM((reps, part, nodes), F32)],
        flops=slot_flops,
        moved=slot_bytes,
    )(index, *all_blocks, held)
    agg = exchange(agg, "rep")

    out_rows, send = call(
        functools.partial(dense_layer, reps),
        [like((nodes, width), BF16), like((reps, part, nodes + width), BF16)],
        [VMEM] * 3,
        flops=6 * nodes * width * width,
        moved=14 * nodes * width,
    )(agg, weight, cotangent)
    arrived = exchange(send, "rep")

    grads = call(
        functools.partial(feature_grads, reps, groups, lists, cap),
        like((groups, part, reps * nodes + width), BF16),
        [SMEM] + [VMEM] * (reps + 1),
        [pltpu.VMEM((groups, reps, part, nodes), F32)],
        flops=slot_flops,
        moved=slot_bytes,
    )(index, *all_blocks, arrived)
    grads = exchange(grads, "blk")

    rows = call(
        functools.partial(sum_groups, reps, groups),
        like((reps, part, nodes + width), BF16),
        [VMEM],
        moved=3 * groups * nodes * width,
    )(grads)
    rows = exchange(rows, "rep")

    grad_feats, grad_weight = call(
        functools.partial(finish, reps),
        [like((nodes, width), F32), like((width, width), F32)],
        [VMEM],
        moved=12 * nodes * width,
    )(rows)
    return (out_rows, grad_weight, grad_feats)


def solution(mesh):
    return jax.shard_map(
        per_device,
        mesh=mesh,
        in_specs=(
            P(("blk", "rep"), None),
            P(),
            P(("blk", "rep"), None),
            P("blk", "rep", None, None, None, None),
            P("blk", "rep", None, None),
            P("blk", "rep", None, None),
            P("blk", "rep", None),
        ),
        out_specs=(P(("blk", "rep"), None), P(), P(("blk", "rep"), None)),
        check_vma=False,
    )
```

```python
import functools

import jax
import jax.numpy as jnp
from jax import lax
from jax.experimental import pallas as pl
from jax.experimental.pallas import tpu as pltpu
from jax.sharding import PartitionSpec as P

F32 = jnp.float32
BF16 = jnp.bfloat16
VMEM = pl.BlockSpec(memory_space=pltpu.VMEM)
SMEM = pl.BlockSpec(memory_space=pltpu.SMEM)
PAD = 16


def shift(array, by):
    peers = lax.axis_size("rep")
    return lax.ppermute(array, "rep", [(i, (i + by) % peers) for i in range(peers)])


def swap(array, bit):
    peers = lax.axis_size("blk")
    return lax.ppermute(array, "blk", [(i, i ^ bit) for i in range(peers)])


def call(body, outs, in_specs, scratch=(), flops=0, moved=0):
    return pl.pallas_call(
        body,
        out_shape=outs,
        in_specs=in_specs,
        out_specs=jax.tree.map(lambda _: VMEM, outs),
        scratch_shapes=list(scratch),
        compiler_params=pltpu.CompilerParams(vmem_limit_bytes=48 * 1024 * 1024),
        cost_estimate=pl.CostEstimate(flops=flops, bytes_accessed=moved, transcendentals=0),
    )


def dot(a, b, a_dim, b_dim):
    return lax.dot_general(a, b, (((a_dim,), (b_dim,)), ((), ())), preferred_element_type=F32)


def member_and(by, reps):
    return lax.rem(lax.axis_index("rep") + by, reps)


def split_features(reps, lists, cap, feats, rows, cols, counts, *rest):
    outs, turned = rest[:-1], rest[-1]
    nodes = feats.shape[0]
    part = feats.shape[1] // reps
    turned[...] = feats[...].astype(F32).T.astype(BF16).reshape(turned.shape)
    lane = lax.broadcasted_iota(jnp.int32, (PAD, nodes), 1)
    index = jnp.zeros((PAD, nodes), jnp.int32)
    slots = lists * cap
    for j in range(lists):
        for c in range(cap):
            k = j * cap + c
            index = jnp.where(lane == k, rows[j, c], index)
            index = jnp.where(lane == slots + k, cols[j, c], index)
        index = jnp.where(lane == 2 * slots + j, counts[j], index)
    index = index.astype(F32).astype(BF16)
    for t in range(reps):
        outs[t][:part] = turned[member_and(t, reps)]
        outs[t][part:] = index


def order_chunks(reps, part, *refs):
    chunks, mine, index = refs[:reps], refs[reps], refs[reps + 1]
    for t in range(reps):
        origin = member_and(reps - t, reps)
        mine[0, origin] = chunks[t][:part]
        index[origin] = chunks[t][part:].astype(F32).astype(jnp.int32)


def join(first, second, out):
    half = first.shape[0]
    out[:half] = first[...]
    out[half:] = second[...]


def slot_of(index, lists, cap, t, j, c):
    k = j * cap + c
    slots = lists * cap
    return index[t, 0, k], index[t, 0, slots + k], c < index[t, 0, 2 * slots + j]


def relative(groups, lists, origin, j):
    mine = lax.axis_index("blk")
    return lax.bitwise_xor(mine, lax.rem(mine + groups - origin * lists - j, groups))


def aggregate(reps, groups, lists, cap, index, *refs):
    blocks = refs[:reps]
    near, far, out, held, total = refs[reps:]
    half = groups // 2
    held[0] = near[...]
    held[1] = far[...]
    total[...] = jnp.zeros_like(total)
    for t in range(reps):
        origin = member_and(reps - t, reps)
        for j in range(lists):
            place = relative(groups, lists, origin, j)
            for c in range(cap):
                row, col, live = slot_of(index, lists, cap, origin, j, c)
                source = held[lax.rem(place, 2), lax.div(place, 2), col]
                product = dot(source, blocks[t][j * cap + c], 1, 1)
                total[row] += jnp.where(live, product, 0.0)
    out[...] = total[...].astype(BF16)


def dense_and_back(reps, groups, lists, cap, index, *refs):
    blocks = refs[:reps]
    chunks = refs[reps : 2 * reps]
    cotangents = refs[2 * reps : 3 * reps]
    weight, out, keep, send = refs[3 * reps : 3 * reps + 4]
    agg, cot, outs, dagg, total = refs[3 * reps + 4 :]
    nodes, width = out.shape
    me = lax.axis_index("rep")
    half = groups // 2
    for t in range(reps):
        origin = member_and(reps - t, reps)
        cot[origin] = cotangents[t][...]
        for b in range(reps):
            agg[b, origin] = chunks[t][b]
    total[...] = jnp.zeros_like(total)
    gw = jnp.zeros((width, width), F32)
    for b in range(reps):
        turned = agg[b].reshape(width, nodes)
        pre = dot(turned, weight[...], 0, 0)
        sigma = jax.nn.sigmoid(pre)
        outs[b] = (pre * sigma).astype(BF16)
        slope = sigma * (1.0 + pre * (1.0 - sigma))
        dpre = (cot[b].astype(F32) * slope).astype(BF16)
        dagg[b] = dot(dpre, weight[...], 1, 1).astype(BF16)
        gw += dot(turned, dpre, 1, 0)
    out[...] = outs[me]
    gw = gw.astype(BF16).reshape(-1, nodes, width)
    keep[half:] = gw.astype(F32)
    send[half:] = gw
    for t in range(reps):
        origin = member_and(reps - t, reps)
        for j in range(lists):
            place = relative(groups, lists, origin, j)
            for c in range(cap):
                row, col, live = slot_of(index, lists, cap, origin, j, c)

                @pl.when(jnp.logical_and(live, col == me))
                def _():
                    total[lax.rem(place, 2), lax.div(place, 2)] += dot(
                        blocks[t][j * cap + c], dagg[row], 0, 0
                    )

    keep[:half] = total[0]
    send[:half] = total[1].astype(BF16)


def add_and_halve(half, keep, arrived, next_keep, next_send):
    next_keep[:half] = keep[:half] + arrived[:half].astype(F32)
    next_send[:half] = (keep[half : 2 * half] + arrived[half : 2 * half].astype(F32)).astype(BF16)
    gw = (keep[2 * half :] + arrived[2 * half :].astype(F32)).astype(BF16)
    next_keep[half:] = gw.astype(F32)
    next_send[half:] = gw


def finish(keep, arrived, grad_feats, grad_weight):
    total = keep[...] + arrived[...].astype(F32)
    grad_feats[...] = total[0]
    grad_weight[...] = total[1:].reshape(grad_weight.shape)


def per_device(feats, weight, cotangent, block_vals, block_rows, block_cols, step_counts):
    reps = lax.axis_size("rep")
    groups = lax.axis_size("blk")
    lists, cap, block = block_vals.shape[2:5]
    nodes, width = feats.shape
    part = width // reps
    extra = width // nodes
    like = jax.ShapeDtypeStruct
    blocks = block_vals.reshape(lists * cap, block, block)

    def over_rep(arrays):
        return [arrays[0]] + [shift(arrays[t], t) for t in range(1, reps)]

    all_blocks = over_rep([blocks] * reps)
    chunks = call(
        functools.partial(split_features, reps, lists, cap),
        [like((part + PAD, nodes), BF16)] * reps,
        [VMEM, SMEM, SMEM, SMEM],
        [pltpu.VMEM((reps, part, nodes), BF16)],
        moved=4 * nodes * width,
    )(feats, block_rows[0, 0], block_cols[0, 0], step_counts[0, 0])
    near, index = call(
        functools.partial(order_chunks, reps, part),
        [like((1, reps, part, nodes), BF16), like((reps, PAD, nodes), jnp.int32)],
        [VMEM] * reps,
        moved=4 * nodes * width,
    )(*over_rep(chunks))
    all_cotangents = over_rep([cotangent] * reps)

    bit = 2
    while bit < groups:
        near = call(
            join,
            like((2 * near.shape[0],) + near.shape[1:], BF16),
            [VMEM] * 2,
            moved=8 * near.size,
        )(near, swap(near, bit))
        bit *= 2
    far = swap(near, 1)
    slot_flops = 2 * groups * cap * part * block * block
    slot_bytes = 2 * (groups * cap * block * block + groups * nodes * width)

    agg = call(
        functools.partial(aggregate, reps, groups, lists, cap),
        like((reps, part, nodes), BF16),
        [SMEM] + [VMEM] * (reps + 2),
        [
            pltpu.VMEM((2, groups // 2, reps, part, nodes), BF16),
            pltpu.VMEM((reps, part, nodes), F32),
        ],
        flops=slot_flops,
        moved=slot_bytes,
    )(index, *all_blocks, near, far)
    aggs = over_rep([agg] * reps)

    half = groups // 2
    out_rows, keep, send = call(
        functools.partial(dense_and_back, reps, groups, lists, cap),
        [
            like((nodes, width), BF16),
            like((half + extra, nodes, width), F32),
            like((half + extra, nodes, width), BF16),
        ],
        [SMEM] + [VMEM] * (3 * reps + 1),
        [
            pltpu.VMEM((reps, reps, part, nodes), BF16),
            pltpu.VMEM((reps, nodes, width), BF16),
            pltpu.VMEM((reps, nodes, width), BF16),
            pltpu.VMEM((reps, nodes, width), BF16),
            pltpu.VMEM((2, half, nodes, width), F32),
        ],
        flops=slot_flops + 6 * reps * nodes * width * width,
        moved=2 * slot_bytes,
    )(index, *all_blocks, *aggs, *all_cotangents, weight)
    arrived = swap(send, 1)
    bit = groups // 2
    while bit > 1:
        half = half // 2
        keep, send = call(
            functools.partial(add_and_halve, half),
            [
                like((half + extra, nodes, width), F32),
                like((half + extra, nodes, width), BF16),
            ],
            [VMEM] * 2,
            moved=12 * (half + extra) * nodes * width,
        )(keep, arrived)
        arrived = swap(send, bit)
        bit = bit // 2

    grad_feats, grad_weight = call(
        finish,
        [like((nodes, width), F32), like((width, width), F32)],
        [VMEM] * 2,
        moved=30 * nodes * width,
    )(keep, arrived)
    return (out_rows, grad_weight, grad_feats)


def solution(mesh):
    return jax.shard_map(
        per_device,
        mesh=mesh,
        in_specs=(
            P(("blk", "rep"), None),
            P(),
            P(("blk", "rep"), None),
            P("blk", "rep", None, None, None, None),
            P("blk", "rep", None, None),
            P("blk", "rep", None, None),
            P("blk", "rep", None),
        ),
        out_specs=(P(("blk", "rep"), None), P(), P(("blk", "rep"), None)),
        check_vma=False,
    )
```

```python
import functools

import jax
import jax.numpy as jnp
from jax import lax
from jax.experimental import pallas as pl
from jax.experimental.pallas import tpu as pltpu
from jax.sharding import PartitionSpec as P

F32 = jnp.float32
BF16 = jnp.bfloat16
VMEM = pl.BlockSpec(memory_space=pltpu.VMEM)
SMEM = pl.BlockSpec(memory_space=pltpu.SMEM)
PAD = 16


def shift(array, by):
    peers = lax.axis_size("rep")
    return lax.ppermute(array, "rep", [(i, (i + by) % peers) for i in range(peers)])


def swap(array, axis, bit):
    peers = lax.axis_size(axis)
    return lax.ppermute(array, axis, [(i, i ^ bit) for i in range(peers)])


def relay(array):
    peers = lax.axis_size("rep")
    below, above = [array], [array]
    for step in range(1, peers):
        up = [(i, i + 1) for i in range(step - 1, peers - 1)]
        down = [(i, i - 1) for i in range(1, peers - step + 1)]
        below.append(lax.ppermute(below[-1], "rep", up))
        above.append(lax.ppermute(above[-1], "rep", down))
    return below + above[1:]


def call(body, outs, in_specs, scratch=(), flops=0, moved=0):
    return pl.pallas_call(
        body,
        out_shape=outs,
        in_specs=in_specs,
        out_specs=jax.tree.map(lambda _: VMEM, outs),
        scratch_shapes=list(scratch),
        compiler_params=pltpu.CompilerParams(vmem_limit_bytes=48 * 1024 * 1024),
        cost_estimate=pl.CostEstimate(flops=flops, bytes_accessed=moved, transcendentals=0),
    )


def dot(a, b, a_dim, b_dim):
    return lax.dot_general(a, b, (((a_dim,), (b_dim,)), ((), ())), preferred_element_type=F32)


def member_and(by, reps):
    return lax.rem(lax.axis_index("rep") + by, reps)


def pack(blocks, cotangent, out):
    slots, block = blocks.shape[:2]
    out[:slots] = blocks[...]
    for k in range(cotangent.shape[1] // block):
        out[slots + k] = cotangent[:, k * block : (k + 1) * block]


def split_features(reps, lists, cap, feats, rows, cols, counts, keep, send, turned):
    nodes = feats.shape[0]
    part = feats.shape[1] // reps
    turned[...] = feats[...].astype(F32).T.astype(BF16).reshape(turned.shape)
    lane = lax.broadcasted_iota(jnp.int32, (PAD, nodes), 1)
    index = jnp.zeros((PAD, nodes), jnp.int32)
    slots = lists * cap
    for j in range(lists):
        for c in range(cap):
            k = j * cap + c
            index = jnp.where(lane == k, rows[j, c], index)
            index = jnp.where(lane == slots + k, cols[j, c], index)
        index = jnp.where(lane == 2 * slots + j, counts[j], index)
    index = index.astype(F32).astype(BF16)
    me = lax.axis_index("rep")
    half = reps // 2
    for d in range(reps):
        out = send if d >= half else keep
        out[d % half, :part] = turned[lax.bitwise_xor(me, d)]
        out[d % half, part:] = index


def regroup(held, gone, keep, arrived, next_keep, next_send):
    half = gone // 2
    for o in range(held):
        for source, base in ((keep, 0), (arrived, held)):
            for d in range(half):
                next_keep[(base + o) * half + d] = source[o * gone + d]
                next_send[(base + o) * half + d] = source[o * gone + half + d]


def order_chunks(reps, part, keep, arrived, mine, index):
    me = lax.axis_index("rep")
    half = reps // 2
    for k in range(reps):
        source = arrived if k >= half else keep
        origin = lax.bitwise_xor(me, origin_bits(k, reps))
        mine[0, origin] = source[k % half, :part]
        index[origin] = source[k % half, part:].astype(F32).astype(jnp.int32)


def origin_bits(k, reps):
    bits, value, origin = reps.bit_length() - 1, k, 0
    for i in range(bits):
        if value >> i & 1:
            origin |= 1 << (bits - 1 - i)
    return origin


def join(first, second, out):
    half = first.shape[0]
    out[:half] = first[...]
    out[half:] = second[...]


def slot_of(index, lists, cap, t, j, c):
    k = j * cap + c
    slots = lists * cap
    return index[t, 0, k], index[t, 0, slots + k], c < index[t, 0, 2 * slots + j]


def relative(groups, lists, origin, j):
    mine = lax.axis_index("blk")
    return lax.bitwise_xor(mine, lax.rem(mine + groups - origin * lists - j, groups))


def aggregate(reps, groups, lists, cap, index, *refs):
    arrays = refs[: 2 * reps - 1]
    near, far, out, blocks, cotangents, held, total = refs[2 * reps - 1 :]
    slots = lists * cap
    block = blocks.shape[2]
    me = lax.axis_index("rep")

    def place_at(origin, array):
        blocks[origin] = array[:slots]
        for k in range(cotangents.shape[2] // block):
            cotangents[origin, :, k * block : (k + 1) * block] = array[slots + k]

    place_at(me, arrays[0])
    for step in range(1, reps):
        pl.when(me >= step)(functools.partial(place_at, me - step, arrays[step]))
        pl.when(me + step < reps)(
            functools.partial(place_at, me + step, arrays[reps - 1 + step])
        )
    held[0] = near[...]
    held[1] = far[...]
    total[...] = jnp.zeros_like(total)
    for origin in range(reps):
        for j in range(lists):
            place = relative(groups, lists, origin, j)
            for c in range(cap):
                row, col, live = slot_of(index, lists, cap, origin, j, c)
                source = held[lax.rem(place, 2), lax.div(place, 2), col]
                product = dot(source, blocks[origin, j * cap + c], 1, 1)
                total[row] += jnp.where(live, product, 0.0)
    out[...] = total[...].astype(BF16)


def dense_layer(reps, *refs):
    chunks = refs[:reps]
    cot, weight, out, dagg, terms, agg, outs = refs[reps:]
    nodes, width = out.shape
    for t in range(reps):
        origin = member_and(reps - t, reps)
        for b in range(reps):
            agg[b, origin] = chunks[t][b]
    gw = jnp.zeros((width, width), F32)
    for b in range(reps):
        turned = agg[b].reshape(width, nodes)
        pre = dot(turned, weight[...], 0, 0)
        sigma = jax.nn.sigmoid(pre)
        outs[b] = (pre * sigma).astype(BF16)
        slope = sigma * (1.0 + pre * (1.0 - sigma))
        dpre = (cot[b].astype(F32) * slope).astype(BF16)
        dagg[b] = dot(dpre, weight[...], 1, 1).astype(BF16)
        gw += dot(turned, dpre, 1, 0)
    out[...] = outs[lax.axis_index("rep")]
    terms[...] = gw.astype(BF16)


def feature_grads(reps, groups, lists, cap, index, blocks, dagg, keep, send, total):
    me = lax.axis_index("rep")
    total[...] = jnp.zeros_like(total)
    for origin in range(reps):
        for j in range(lists):
            place = relative(groups, lists, origin, j)
            for c in range(cap):
                row, col, live = slot_of(index, lists, cap, origin, j, c)

                @pl.when(jnp.logical_and(live, col == me))
                def _():
                    total[lax.rem(place, 2), lax.div(place, 2)] += dot(
                        blocks[origin, j * cap + c], dagg[row], 0, 0
                    )

    keep[...] = total[0]
    send[...] = total[1].astype(BF16)


def add_terms(mine, arrived, out):
    out[...] = (mine[...].astype(F32) + arrived[...].astype(F32)).astype(out.dtype)


def add_and_halve(half, keep, arrived, next_keep, next_send):
    next_keep[...] = keep[:half] + arrived[:half].astype(F32)
    next_send[...] = (keep[half:] + arrived[half:].astype(F32)).astype(BF16)


def add_last(keep, arrived, grad_feats):
    grad_feats[...] = keep[0] + arrived[0].astype(F32)


def per_device(feats, weight, cotangent, block_vals, block_rows, block_cols, step_counts):
    reps = lax.axis_size("rep")
    groups = lax.axis_size("blk")
    lists, cap, block = block_vals.shape[2:5]
    nodes, width = feats.shape
    part = width // reps
    extra = width // block
    slots = lists * cap
    like = jax.ShapeDtypeStruct

    packed = call(
        pack,
        like((slots + extra, block, block), BF16),
        [VMEM] * 2,
        moved=4 * (slots + extra) * block * block,
    )(block_vals.reshape(slots, block, block), cotangent)
    relayed = relay(packed)

    piece = like((reps // 2, part + PAD, nodes), BF16)
    keep, send = call(
        functools.partial(split_features, reps, lists, cap),
        [piece] * 2,
        [VMEM, SMEM, SMEM, SMEM],
        [pltpu.VMEM((reps, part, nodes), BF16)],
        moved=4 * nodes * width,
    )(feats, block_rows[0, 0], block_cols[0, 0], step_counts[0, 0])
    bit, origins = reps // 2, 1
    arrived = swap(send, "rep", bit)
    while bit > 1:
        keep, send = call(
            functools.partial(regroup, origins, bit),
            [piece] * 2,
            [VMEM] * 2,
            moved=4 * nodes * width,
        )(keep, arrived)
        bit, origins = bit // 2, origins * 2
        arrived = swap(send, "rep", bit)
    near, index = call(
        functools.partial(order_chunks, reps, part),
        [like((1, reps, part, nodes), BF16), like((reps, PAD, nodes), jnp.int32)],
        [VMEM] * 2,
        moved=4 * nodes * width,
    )(keep, arrived)

    bit = 2
    while bit < groups:
        near = call(
            join,
            like((2 * near.shape[0],) + near.shape[1:], BF16),
            [VMEM] * 2,
            moved=8 * near.size,
        )(near, swap(near, "blk", bit))
        bit *= 2
    far = swap(near, "blk", 1)
    slot_flops = 2 * groups * cap * part * block * block
    slot_bytes = 2 * (groups * cap * block * block + groups * nodes * width)

    agg, blocks, cotangents = call(
        functools.partial(aggregate, reps, groups, lists, cap),
        [
            like((reps, part, nodes), BF16),
            like((reps, slots, block, block), BF16),
            like((reps, nodes, width), BF16),
        ],
        [SMEM] + [VMEM] * (2 * reps + 1),
        [
            pltpu.VMEM((2, groups // 2, reps, part, nodes), BF16),
            pltpu.VMEM((reps, part, nodes), F32),
        ],
        flops=slot_flops,
        moved=slot_bytes,
    )(index, *relayed, near, far)
    aggs = [agg] + [shift(agg, t) for t in range(1, reps)]

    out_rows, dagg, terms = call(
        functools.partial(dense_layer, reps),
        [
            like((nodes, width), BF16),
            like((reps, nodes, width), BF16),
            like((width, width), BF16),
        ],
        [VMEM] * (reps + 2),
        [
            pltpu.VMEM((reps, reps, part, nodes), BF16),
            pltpu.VMEM((reps, nodes, width), BF16),
        ],
        flops=6 * reps * nodes * width * width,
        moved=2 * reps * 5 * nodes * width,
    )(*aggs, cotangents, weight)

    half = groups // 2
    keep, send = call(
        functools.partial(feature_grads, reps, groups, lists, cap),
        [like((half, nodes, width), F32), like((half, nodes, width), BF16)],
        [SMEM] + [VMEM] * 2,
        [pltpu.VMEM((2, half, nodes, width), F32)],
        flops=slot_flops,
        moved=slot_bytes,
    )(index, blocks, dagg)

    bit = 1
    while bit < groups:
        other = swap(terms, "blk", bit)
        bit *= 2
        terms = call(
            add_terms,
            like((width, width), BF16 if bit < groups else F32),
            [VMEM] * 2,
            moved=6 * width * width,
        )(terms, other)

    arrived = swap(send, "blk", 1)
    bit = groups // 2
    while bit > 1:
        half = half // 2
        keep, send = call(
            functools.partial(add_and_halve, half),
            [like((half, nodes, width), F32), like((half, nodes, width), BF16)],
            [VMEM] * 2,
            moved=12 * half * nodes * width,
        )(keep, arrived)
        arrived = swap(send, "blk", bit)
        bit = bit // 2
    grad_feats = call(
        add_last, like((nodes, width), F32), [VMEM] * 2, moved=10 * nodes * width
    )(keep, arrived)
    return (out_rows, terms, grad_feats)


def solution(mesh):
    return jax.shard_map(
        per_device,
        mesh=mesh,
        in_specs=(
            P(("blk", "rep"), None),
            P(),
            P(("blk", "rep"), None),
            P("blk", "rep", None, None, None, None),
            P("blk", "rep", None, None),
            P("blk", "rep", None, None),
            P("blk", "rep", None),
        ),
        out_specs=(P(("blk", "rep"), None), P(), P(("blk", "rep"), None)),
        check_vma=False,
    )
```

```python
import functools

import jax
import jax.numpy as jnp
from jax import lax
from jax.experimental import pallas as pl
from jax.experimental.pallas import tpu as pltpu
from jax.sharding import PartitionSpec as P

F32 = jnp.float32
BF16 = jnp.bfloat16
VMEM = pl.BlockSpec(memory_space=pltpu.VMEM)
SMEM = pl.BlockSpec(memory_space=pltpu.SMEM)
PAD = 16


def shift(array, by):
    peers = lax.axis_size("rep")
    return lax.ppermute(array, "rep", [(i, (i + by) % peers) for i in range(peers)])


def swap(array, axis, bit):
    peers = lax.axis_size(axis)
    return lax.ppermute(array, axis, [(i, i ^ bit) for i in range(peers)])


def call(body, outs, in_specs, scratch=(), flops=0, moved=0):
    return pl.pallas_call(
        body,
        out_shape=outs,
        in_specs=in_specs,
        out_specs=jax.tree.map(lambda _: VMEM, outs),
        scratch_shapes=list(scratch),
        compiler_params=pltpu.CompilerParams(vmem_limit_bytes=48 * 1024 * 1024),
        cost_estimate=pl.CostEstimate(flops=flops, bytes_accessed=moved, transcendentals=0),
    )


def dot(a, b, a_dim, b_dim):
    return lax.dot_general(a, b, (((a_dim,), (b_dim,)), ((), ())), preferred_element_type=F32)


def member_and(by, reps):
    return lax.rem(lax.axis_index("rep") + by, reps)


def pack(blocks, cotangent, out):
    slots, block = blocks.shape[:2]
    for q in range(out.shape[0]):
        out[q, :slots] = blocks[...]
        for k in range(cotangent.shape[1] // block):
            out[q, slots + k] = cotangent[:, k * block : (k + 1) * block]


def split_features(reps, lists, cap, feats, rows, cols, counts, keep, send, turned):
    nodes = feats.shape[0]
    part = feats.shape[1] // reps
    turned[...] = feats[...].astype(F32).T.astype(BF16).reshape(turned.shape)
    lane = lax.broadcasted_iota(jnp.int32, (PAD, nodes), 1)
    index = jnp.zeros((PAD, nodes), jnp.int32)
    slots = lists * cap
    for j in range(lists):
        for c in range(cap):
            k = j * cap + c
            index = jnp.where(lane == k, rows[j, c], index)
            index = jnp.where(lane == slots + k, cols[j, c], index)
        index = jnp.where(lane == 2 * slots + j, counts[j], index)
    index = index.astype(F32).astype(BF16)
    me = lax.axis_index("rep")
    half = reps // 2
    for d in range(reps):
        out = send if d >= half else keep
        out[d % half, :part] = turned[lax.bitwise_xor(me, d)]
        out[d % half, part:] = index


def regroup(held, gone, keep, arrived, next_keep, next_send):
    half = gone // 2
    for o in range(held):
        for source, base in ((keep, 0), (arrived, held)):
            for d in range(half):
                next_keep[(base + o) * half + d] = source[o * gone + d]
                next_send[(base + o) * half + d] = source[o * gone + half + d]


def order_chunks(reps, part, keep, arrived, mine, index):
    me = lax.axis_index("rep")
    half = reps // 2
    for k in range(reps):
        source = arrived if k >= half else keep
        origin = lax.bitwise_xor(me, origin_bits(k, reps))
        mine[origin] = source[k % half, :part]
        index[origin] = source[k % half, part:].astype(F32).astype(jnp.int32)


def origin_bits(k, reps):
    bits, value, origin = reps.bit_length() - 1, k, 0
    for i in range(bits):
        if value >> i & 1:
            origin |= 1 << (bits - 1 - i)
    return origin


def join(*refs):
    out = refs[-1]
    for k, ref in enumerate(refs[:-1]):
        out[k] = ref[...]


def slot_of(index, lists, cap, t, j, c):
    k = j * cap + c
    slots = lists * cap
    return index[t, 0, k], index[t, 0, slots + k], c < index[t, 0, 2 * slots + j]


def relative(groups, offset):
    mine = lax.axis_index("blk")
    return lax.bitwise_xor(mine, lax.rem(mine + groups - offset, groups))


def aggregate(reps, groups, lists, cap, index, blocks, near, far, out, total):
    total[...] = jnp.zeros_like(total)
    for origin in range(reps):
        for j in range(lists):
            offset = origin * lists + j
            held = far if offset % 2 else near
            place = lax.div(relative(groups, offset), 2)
            for c in range(cap):
                row, col, live = slot_of(index, lists, cap, origin, j, c)
                product = dot(held[place, col], blocks[origin, j * cap + c], 1, 1)
                total[row] += jnp.where(live, product, 0.0)
    out[...] = total[...].astype(BF16)


def dense_layer(reps, *refs):
    chunks = refs[:reps]
    packed, weight, out, dagg, terms, agg, outs = refs[reps:]
    nodes, width = out.shape
    slots = packed.shape[1] - width // packed.shape[3]
    for t in range(reps):
        origin = member_and(reps - t, reps)
        for b in range(reps):
            agg[b, origin] = chunks[t][b]
    gw = jnp.zeros((width, width), F32)
    for b in range(reps):
        turned = agg[b].reshape(width, nodes)
        pre = dot(turned, weight[...], 0, 0)
        sigma = jax.nn.sigmoid(pre)
        outs[b] = (pre * sigma).astype(BF16)
        slope = sigma * (1.0 + pre * (1.0 - sigma))
        cot = jnp.concatenate(
            [packed[b, k] for k in range(slots, packed.shape[1])], axis=1
        ).astype(F32)
        dpre = (cot * slope).astype(BF16)
        dagg[b] = dot(dpre, weight[...], 1, 1).astype(BF16)
        gw += dot(turned, dpre, 1, 0)
    out[...] = outs[lax.axis_index("rep")]
    terms[...] = gw.astype(BF16)


def feature_grads(reps, groups, lists, cap, index, blocks, dagg, terms, keep, send, total):
    me = lax.axis_index("rep")
    half = groups // 2
    keep[...] = jnp.zeros_like(keep)
    total[...] = jnp.zeros_like(total)
    for origin in range(reps):
        for j in range(lists):
            offset = origin * lists + j
            target = total if offset % 2 else keep
            place = lax.div(relative(groups, offset), 2)
            for c in range(cap):
                row, col, live = slot_of(index, lists, cap, origin, j, c)

                @pl.when(jnp.logical_and(live, col == me))
                def _():
                    target[place] += dot(blocks[origin, j * cap + c], dagg[row], 0, 0)

    send[:half] = total[...].astype(BF16)
    send[half:] = terms[...].reshape(-1, *send.shape[1:])


def add_core(half, keep, terms, arrived, own, gw, *sends):
    own[...] = keep[0] + arrived[0].astype(F32)
    for k in range(1, half):
        sends[k - 1][...] = (keep[k] + arrived[k].astype(F32)).astype(BF16)
    other = arrived[half:].reshape(terms.shape).astype(F32)
    gw[...] = (terms[...].astype(F32) + other).astype(BF16)


def add_terms(mine, arrived, out):
    out[...] = (mine[...].astype(F32) + arrived[...].astype(F32)).astype(out.dtype)


def add_last(own, *refs):
    total = own[...]
    for ref in refs[:-1]:
        total += ref[...].astype(F32)
    refs[-1][...] = total


def per_device(feats, weight, cotangent, block_vals, block_rows, block_cols, step_counts):
    reps = lax.axis_size("rep")
    groups = lax.axis_size("blk")
    lists, cap, block = block_vals.shape[2:5]
    nodes, width = feats.shape
    part = width // reps
    extra = width // block
    slots = lists * cap
    half = groups // 2
    like = jax.ShapeDtypeStruct

    packed = call(
        pack,
        like((reps, slots + extra, block, block), BF16),
        [VMEM] * 2,
        moved=2 * (1 + reps) * (slots + extra) * block * block,
    )(block_vals.reshape(slots, block, block), cotangent)
    packed = lax.all_to_all(packed, "rep", 0, 0, tiled=True)

    piece = like((reps // 2, part + PAD, nodes), BF16)
    keep, send = call(
        functools.partial(split_features, reps, lists, cap),
        [piece] * 2,
        [VMEM, SMEM, SMEM, SMEM],
        [pltpu.VMEM((reps, part, nodes), BF16)],
        moved=4 * nodes * width,
    )(feats, block_rows[0, 0], block_cols[0, 0], step_counts[0, 0])
    bit, origins = reps // 2, 1
    arrived = swap(send, "rep", bit)
    while bit > 1:
        keep, send = call(
            functools.partial(regroup, origins, bit),
            [piece] * 2,
            [VMEM] * 2,
            moved=4 * nodes * width,
        )(keep, arrived)
        bit, origins = bit // 2, origins * 2
        arrived = swap(send, "rep", bit)
    mine, index = call(
        functools.partial(order_chunks, reps, part),
        [like((reps, part, nodes), BF16), like((reps, PAD, nodes), jnp.int32)],
        [VMEM] * 2,
        moved=4 * nodes * width,
    )(keep, arrived)

    near = call(
        join,
        like((half, reps, part, nodes), BF16),
        [VMEM] * half,
        moved=4 * half * nodes * width,
    )(mine, *[swap(mine, "blk", 2 * k) for k in range(1, half)])
    far = swap(near, "blk", 1)
    slot_flops = 2 * groups * cap * part * block * block
    slot_bytes = 2 * (groups * cap * block * block + groups * nodes * width)

    agg = call(
        functools.partial(aggregate, reps, groups, lists, cap),
        like((reps, part, nodes), BF16),
        [SMEM] + [VMEM] * 3,
        [pltpu.VMEM((reps, part, nodes), F32)],
        flops=slot_flops,
        moved=slot_bytes,
    )(index, packed, near, far)
    aggs = [agg] + [shift(agg, t) for t in range(1, reps)]

    out_rows, dagg, terms = call(
        functools.partial(dense_layer, reps),
        [
            like((nodes, width), BF16),
            like((reps, nodes, width), BF16),
            like((width, width), BF16),
        ],
        [VMEM] * (reps + 2),
        [
            pltpu.VMEM((reps, reps, part, nodes), BF16),
            pltpu.VMEM((reps, nodes, width), BF16),
        ],
        flops=6 * reps * nodes * width * width,
        moved=2 * reps * 5 * nodes * width,
    )(*aggs, packed, weight)

    keep, send = call(
        functools.partial(feature_grads, reps, groups, lists, cap),
        [
            like((half, nodes, width), F32),
            like((half + width // nodes, nodes, width), BF16),
        ],
        [SMEM] + [VMEM] * 3,
        [pltpu.VMEM((half, nodes, width), F32)],
        flops=slot_flops,
        moved=slot_bytes,
    )(index, packed, dagg, terms)
    own, terms, *sends = call(
        functools.partial(add_core, half),
        [like((nodes, width), F32), like((width, width), BF16)]
        + [like((nodes, width), BF16)] * (half - 1),
        [VMEM] * 3,
        moved=10 * half * nodes * width,
    )(keep, terms, swap(send, "blk", 1))
    rest = [swap(sends[k - 1], "blk", 2 * k) for k in range(1, half)]

    bit = 2
    while bit < groups:
        other = swap(terms, "blk", bit)
        bit *= 2
        terms = call(
            add_terms,
            like((width, width), BF16 if bit < groups else F32),
            [VMEM] * 2,
            moved=6 * width * width,
        )(terms, other)
    grad_feats = call(
        add_last,
        like((nodes, width), F32),
        [VMEM] * half,
        moved=(6 + 2 * half) * nodes * width,
    )(own, *rest)
    return (out_rows, terms, grad_feats)


def solution(mesh):
    return jax.shard_map(
        per_device,
        mesh=mesh,
        in_specs=(
            P(("blk", "rep"), None),
            P(),
            P(("blk", "rep"), None),
            P("blk", "rep", None, None, None, None),
            P("blk", "rep", None, None),
            P("blk", "rep", None, None),
            P("blk", "rep", None),
        ),
        out_specs=(P(("blk", "rep"), None), P(), P(("blk", "rep"), None)),
        check_vma=False,
    )
```

```python
import functools

import jax
import jax.numpy as jnp
from jax import lax
from jax.experimental import pallas as pl
from jax.experimental.pallas import tpu as pltpu
from jax.sharding import PartitionSpec as P

F32 = jnp.float32
BF16 = jnp.bfloat16
VMEM = pl.BlockSpec(memory_space=pltpu.VMEM)
SMEM = pl.BlockSpec(memory_space=pltpu.SMEM)
PAD = 16


def swap(array, axis, bit):
    peers = lax.axis_size(axis)
    return lax.ppermute(array, axis, [(i, i ^ bit) for i in range(peers)])


def spread(array):
    reps = lax.axis_size("rep")
    held = {0: array}
    bit = reps // 2
    while bit:
        held.update({x | bit: swap(part, "rep", bit) for x, part in held.items()})
        bit //= 2
    return [held[x] for x in range(reps)]


def call(body, outs, in_specs, scratch=(), flops=0, moved=0):
    return pl.pallas_call(
        body,
        out_shape=outs,
        in_specs=in_specs,
        out_specs=jax.tree.map(lambda _: VMEM, outs),
        scratch_shapes=list(scratch),
        compiler_params=pltpu.CompilerParams(vmem_limit_bytes=48 * 1024 * 1024),
        cost_estimate=pl.CostEstimate(flops=flops, bytes_accessed=moved, transcendentals=0),
    )


def dot(a, b, a_dim, b_dim):
    return lax.dot_general(a, b, (((a_dim,), (b_dim,)), ((), ())), preferred_element_type=F32)


def other(axis, by):
    return lax.bitwise_xor(lax.axis_index(axis), by)


def split_features(reps, lists, cap, feats, rows, cols, counts, *rest):
    outs, turned = rest[:-1], rest[-1]
    nodes = feats.shape[0]
    part = feats.shape[1] // reps
    turned[...] = feats[...].astype(F32).T.astype(BF16).reshape(turned.shape)
    lane = lax.broadcasted_iota(jnp.int32, (PAD, nodes), 1)
    index = jnp.zeros((PAD, nodes), jnp.int32)
    slots = lists * cap
    for j in range(lists):
        for c in range(cap):
            k = j * cap + c
            index = jnp.where(lane == k, rows[j, c], index)
            index = jnp.where(lane == slots + k, cols[j, c], index)
        index = jnp.where(lane == 2 * slots + j, counts[j], index)
    index = index.astype(F32).astype(BF16)
    for x in range(reps):
        outs[x][:part] = turned[other("rep", x)]
        outs[x][part:] = index


def order_chunks(reps, part, *refs):
    chunks, unread, mine, index = refs[:reps], refs[reps], refs[-2], refs[-1]
    for x in range(reps):
        mine[other("rep", x)] = chunks[x][:part]
        index[x] = chunks[x][part:].astype(F32).astype(jnp.int32)


def join(*refs):
    out = refs[-1]
    for k, ref in enumerate(refs[:-1]):
        out[k] = ref[...]


def slot_of(index, lists, cap, t, j, c):
    k = j * cap + c
    slots = lists * cap
    return index[t, 0, k], index[t, 0, slots + k], c < index[t, 0, 2 * slots + j]


def relative(groups, lists, x, j):
    mine = lax.axis_index("blk")
    offset = other("rep", x) * lists + j
    return lax.div(lax.bitwise_xor(mine, lax.rem(mine + groups - offset, groups)), 2)


def aggregate(reps, groups, lists, cap, index, *refs):
    blocks = refs[:reps]
    near, far, out, total = refs[reps:]
    total[...] = jnp.zeros_like(total)
    for x in range(reps):
        for j in range(lists):
            held = far if j % 2 else near
            place = relative(groups, lists, x, j)
            for c in range(cap):
                row, col, live = slot_of(index, lists, cap, x, j, c)
                product = dot(held[place, col], blocks[x][j * cap + c], 1, 1)
                total[row] += jnp.where(live, product, 0.0)
    out[...] = total[...].astype(BF16)


def dense_layer(reps, *refs):
    chunks = refs[:reps]
    cotangents = refs[reps : 2 * reps]
    weight, out, dagg, terms, agg, cot, outs = refs[2 * reps :]
    nodes, width = out.shape
    for x in range(reps):
        origin = other("rep", x)
        cot[origin] = cotangents[x][...]
        for b in range(reps):
            agg[b, origin] = chunks[x][b]
    gw = jnp.zeros((width, width), F32)
    for b in range(reps):
        turned = agg[b].reshape(width, nodes)
        pre = dot(turned, weight[...], 0, 0)
        sigma = jax.nn.sigmoid(pre)
        outs[b] = (pre * sigma).astype(BF16)
        slope = sigma * (1.0 + pre * (1.0 - sigma))
        dpre = (cot[b].astype(F32) * slope).astype(BF16)
        dagg[b] = dot(dpre, weight[...], 1, 1).astype(BF16)
        gw += dot(turned, dpre, 1, 0)
    out[...] = outs[lax.axis_index("rep")]
    terms[...] = gw.astype(BF16).reshape(terms.shape)


def feature_grads(reps, groups, lists, cap, index, *refs):
    blocks = refs[:reps]
    dagg, terms, keep, send, total = refs[reps:]
    me = lax.axis_index("rep")
    half = groups // 2
    keep[...] = jnp.zeros_like(keep)
    total[...] = jnp.zeros_like(total)
    for x in range(reps):
        for j in range(lists):
            target = total if j % 2 else keep
            place = relative(groups, lists, x, j)
            for c in range(cap):
                row, col, live = slot_of(index, lists, cap, x, j, c)

                @pl.when(jnp.logical_and(live, col == me))
                def _():
                    target[place] += dot(blocks[x][j * cap + c], dagg[row], 0, 0)

    send[:half] = total[...].astype(BF16)
    core = lax.rem(lax.axis_index("blk"), 2)
    send[half:] = terms[1 - core].reshape(-1, *send.shape[1:])


def add_core(half, keep, terms, arrived, own, own_terms, *sends):
    nodes = own.shape[0]
    own[...] = keep[0] + arrived[0].astype(F32)
    core = lax.rem(lax.axis_index("blk"), 2)
    mine = terms[core].astype(F32)
    gw = (mine + arrived[half:].reshape(mine.shape).astype(F32)).astype(BF16)
    own_terms[...] = gw
    for k in range(1, half):
        sends[k - 1][:nodes] = (keep[k] + arrived[k].astype(F32)).astype(BF16)
        sends[k - 1][nodes:] = gw


def add_chips(half, own, own_terms, *refs):
    parts, grads, terms, held = refs[: half - 1], refs[-3], refs[-2], refs[-1]
    nodes = own.shape[0]
    chip = lax.div(lax.axis_index("blk"), 2)
    total = own[...]
    held[chip] = own_terms[...].astype(F32)
    for k in range(1, half):
        total += parts[k - 1][:nodes].astype(F32)
        held[lax.bitwise_xor(chip, k)] = parts[k - 1][nodes:].astype(F32)
    grads[...] = total
    gw = held[0]
    for k in range(1, half):
        gw += held[k]
    terms[...] = gw


def join_cores(mine, arrived, out):
    core = lax.rem(lax.axis_index("blk"), 2)
    rows = mine.shape[0]
    out[pl.ds(pl.multiple_of(core * rows, rows), rows), :] = mine[...]
    out[pl.ds(pl.multiple_of((1 - core) * rows, rows), rows), :] = arrived[...]


def per_device(feats, weight, cotangent, block_vals, block_rows, block_cols, step_counts):
    reps = lax.axis_size("rep")
    groups = lax.axis_size("blk")
    lists, cap, block = block_vals.shape[2:5]
    nodes, width = feats.shape
    part = width // reps
    slots = lists * cap
    half = groups // 2
    like = jax.ShapeDtypeStruct

    def direct(arrays):
        return [arrays[0]] + [swap(arrays[x], "rep", x) for x in range(1, reps)]

    blocks = spread(block_vals.reshape(slots, block, block))
    chunks = call(
        functools.partial(split_features, reps, lists, cap),
        [like((part + PAD, nodes), BF16)] * reps,
        [VMEM, SMEM, SMEM, SMEM],
        [pltpu.VMEM((reps, part, nodes), BF16)],
        moved=4 * nodes * width,
    )(feats, block_rows[0, 0], block_cols[0, 0], step_counts[0, 0])
    mine, index = call(
        functools.partial(order_chunks, reps, part),
        [like((reps, part, nodes), BF16), like((reps, PAD, nodes), jnp.int32)],
        [VMEM] * reps + [pl.BlockSpec(memory_space=pl.ANY)],
        moved=4 * nodes * width,
    )(*direct(chunks), blocks[1])

    near = call(
        join,
        like((half, reps, part, nodes), BF16),
        [VMEM] * half,
        moved=4 * half * nodes * width,
    )(mine, *[swap(mine, "blk", 2 * k) for k in range(1, half)])
    far = swap(near, "blk", 1)
    slot_flops = 2 * groups * cap * part * block * block
    slot_bytes = 2 * (groups * cap * block * block + groups * nodes * width)

    agg = call(
        functools.partial(aggregate, reps, groups, lists, cap),
        like((reps, part, nodes), BF16),
        [SMEM] + [VMEM] * (reps + 2),
        [pltpu.VMEM((reps, part, nodes), F32)],
        flops=slot_flops,
        moved=slot_bytes,
    )(index, *blocks, near, far)

    out_rows, dagg, terms = call(
        functools.partial(dense_layer, reps),
        [
            like((nodes, width), BF16),
            like((reps, nodes, width), BF16),
            like((2, width // 2, width), BF16),
        ],
        [VMEM] * (2 * reps + 1),
        [
            pltpu.VMEM((reps, reps, part, nodes), BF16),
            pltpu.VMEM((reps, nodes, width), BF16),
            pltpu.VMEM((reps, nodes, width), BF16),
        ],
        flops=6 * reps * nodes * width * width,
        moved=2 * reps * 5 * nodes * width,
    )(*direct([agg] * reps), *spread(cotangent), weight)

    keep, send = call(
        functools.partial(feature_grads, reps, groups, lists, cap),
        [
            like((half, nodes, width), F32),
            like((half + width // 2 // nodes, nodes, width), BF16),
        ],
        [SMEM] + [VMEM] * (reps + 2),
        [pltpu.VMEM((half, nodes, width), F32)],
        flops=slot_flops,
        moved=slot_bytes,
    )(index, *blocks, dagg, terms)
    own, own_terms, *sends = call(
        functools.partial(add_core, half),
        [like((nodes, width), F32), like((width // 2, width), BF16)]
        + [like((nodes + width // 2, width), BF16)] * (half - 1),
        [VMEM] * 3,
        moved=10 * half * nodes * width,
    )(keep, terms, swap(send, "blk", 1))
    grad_feats, terms = call(
        functools.partial(add_chips, half),
        [like((nodes, width), F32), like((width // 2, width), F32)],
        [VMEM] * (half + 1),
        [pltpu.VMEM((half, width // 2, width), F32)],
        moved=8 * half * nodes * width,
    )(own, own_terms, *[swap(sends[k - 1], "blk", 2 * k) for k in range(1, half)])
    grad_weight = call(
        join_cores, like((width, width), F32), [VMEM] * 2, moved=8 * width * width
    )(terms, swap(terms, "blk", 1))
    return (out_rows, grad_weight, grad_feats)


def solution(mesh):
    return jax.shard_map(
        per_device,
        mesh=mesh,
        in_specs=(
            P(("blk", "rep"), None),
            P(),
            P(("blk", "rep"), None),
            P("blk", "rep", None, None, None, None),
            P("blk", "rep", None, None),
            P("blk", "rep", None, None),
            P("blk", "rep", None),
        ),
        out_specs=(P(("blk", "rep"), None), P(), P(("blk", "rep"), None)),
        check_vma=False,
    )
```

```python
import functools

import jax
import jax.numpy as jnp
from jax import lax
from jax.experimental import pallas as pl
from jax.experimental.pallas import tpu as pltpu
from jax.sharding import PartitionSpec as P

F32 = jnp.float32
BF16 = jnp.bfloat16
VMEM = pl.BlockSpec(memory_space=pltpu.VMEM)
SMEM = pl.BlockSpec(memory_space=pltpu.SMEM)
PAD = 16


def swap(array, axis, bit):
    peers = lax.axis_size(axis)
    return lax.ppermute(array, axis, [(i, i ^ bit) for i in range(peers)])


def spread(array, last=1):
    reps = lax.axis_size("rep")
    held = {0: array}
    bit = reps // 2
    while bit >= last:
        held.update({x | bit: swap(part, "rep", bit) for x, part in held.items()})
        bit //= 2
    return [held[x] for x in sorted(held)]


def call(body, outs, in_specs, scratch=(), flops=0, moved=0):
    return pl.pallas_call(
        body,
        out_shape=outs,
        in_specs=in_specs,
        out_specs=jax.tree.map(lambda _: VMEM, outs),
        scratch_shapes=list(scratch),
        compiler_params=pltpu.CompilerParams(vmem_limit_bytes=48 * 1024 * 1024),
        cost_estimate=pl.CostEstimate(flops=flops, bytes_accessed=moved, transcendentals=0),
    )


def dot(a, b, a_dim, b_dim):
    return lax.dot_general(a, b, (((a_dim,), (b_dim,)), ((), ())), preferred_element_type=F32)


def other(axis, by):
    return lax.bitwise_xor(lax.axis_index(axis), by)


def split_features(reps, lists, cap, feats, rows, cols, counts, *rest):
    outs, turned = rest[:-1], rest[-1]
    nodes = feats.shape[0]
    part = feats.shape[1] // reps
    turned[...] = feats[...].astype(F32).T.astype(BF16).reshape(turned.shape)
    lane = lax.broadcasted_iota(jnp.int32, (PAD, nodes), 1)
    index = jnp.zeros((PAD, nodes), jnp.int32)
    slots = lists * cap
    for j in range(lists):
        for c in range(cap):
            k = j * cap + c
            index = jnp.where(lane == k, rows[j, c], index)
            index = jnp.where(lane == slots + k, cols[j, c], index)
        index = jnp.where(lane == 2 * slots + j, counts[j], index)
    index = index.astype(F32).astype(BF16)
    for x in range(reps):
        outs[x][:part] = turned[other("rep", x)]
        outs[x][part:] = index


def order_chunks(reps, part, *refs):
    copies = reps // 2
    chunks, sources, unread = refs[:reps], refs[reps : reps + copies], refs[reps + copies]
    mine, index = refs[reps + copies + 1 : reps + copies + 3]
    for source, target in zip(sources, refs[reps + copies + 3 :]):
        target[...] = source[...]
    for x in range(reps):
        mine[other("rep", x)] = chunks[x][:part]
        index[x] = chunks[x][part:].astype(F32).astype(jnp.int32)


def join(half, *refs):
    out, pairs = refs[-2:]
    for k, ref in enumerate(refs[:half]):
        out[k] = ref[...]
    for k in range(pairs.shape[0]):
        pairs[k] = refs[half + k][...]


def slot_of(index, lists, cap, t, j, c):
    k = j * cap + c
    slots = lists * cap
    return index[t, 0, k], index[t, 0, slots + k], c < index[t, 0, 2 * slots + j]


def relative(groups, lists, x, j):
    mine = lax.axis_index("blk")
    offset = other("rep", x) * lists + j
    return lax.div(lax.bitwise_xor(mine, lax.rem(mine + groups - offset, groups)), 2)


def aggregate(reps, groups, lists, cap, index, *refs):
    blocks = refs[:reps]
    near, far, out, total = refs[reps:]
    total[...] = jnp.zeros_like(total)
    for x in range(reps):
        for j in range(lists):
            held = far if j % 2 else near
            place = relative(groups, lists, x, j)
            for c in range(cap):
                row, col, live = slot_of(index, lists, cap, x, j, c)
                product = dot(held[place, col], blocks[x][j * cap + c], 1, 1)
                total[row] += jnp.where(live, product, 0.0)
    out[...] = total[...].astype(BF16)


def dense_layer(reps, *refs):
    chunks = refs[:reps]
    cotangents = refs[reps : reps + 2]
    weight, out, dagg, terms, agg, cot, outs = refs[reps + 2 :]
    nodes, width = out.shape
    for x in range(reps):
        origin = other("rep", x)
        cot[origin] = cotangents[x % 2][x // 2]
        for b in range(reps):
            agg[b, origin] = chunks[x][b]
    gw = jnp.zeros((width, width), F32)
    for b in range(reps):
        turned = agg[b].reshape(width, nodes)
        pre = dot(turned, weight[...], 0, 0)
        sigma = jax.nn.sigmoid(pre)
        outs[b] = (pre * sigma).astype(BF16)
        slope = sigma * (1.0 + pre * (1.0 - sigma))
        dpre = (cot[b].astype(F32) * slope).astype(BF16)
        dagg[b] = dot(dpre, weight[...], 1, 1).astype(BF16)
        gw += dot(turned, dpre, 1, 0)
    out[...] = outs[lax.axis_index("rep")]
    terms[...] = gw.astype(BF16).reshape(terms.shape)


def feature_grads(reps, groups, lists, cap, index, *refs):
    blocks = refs[:reps]
    dagg, terms, keep, send, total = refs[reps:]
    me = lax.axis_index("rep")
    half = groups // 2
    keep[...] = jnp.zeros_like(keep)
    total[...] = jnp.zeros_like(total)
    for x in range(reps):
        for j in range(lists):
            target = total if j % 2 else keep
            place = relative(groups, lists, x, j)
            for c in range(cap):
                row, col, live = slot_of(index, lists, cap, x, j, c)

                @pl.when(jnp.logical_and(live, col == me))
                def _():
                    target[place] += dot(blocks[x][j * cap + c], dagg[row], 0, 0)

    send[:half] = total[...].astype(BF16)
    core = lax.rem(lax.axis_index("blk"), 2)
    send[half:] = terms[1 - core].reshape(-1, *send.shape[1:])


def add_core(half, keep, terms, arrived, own, own_terms, *sends):
    nodes = own.shape[0]
    own[...] = keep[0] + arrived[0].astype(F32)
    core = lax.rem(lax.axis_index("blk"), 2)
    mine = terms[core].astype(F32)
    gw = (mine + arrived[half:].reshape(mine.shape).astype(F32)).astype(BF16)
    own_terms[...] = gw
    for k in range(1, half):
        sends[k - 1][:nodes] = (keep[k] + arrived[k].astype(F32)).astype(BF16)
        sends[k - 1][nodes:] = gw


def add_chips(half, own, own_terms, *refs):
    parts, grads, terms, held = refs[: half - 1], refs[-3], refs[-2], refs[-1]
    nodes = own.shape[0]
    chip = lax.div(lax.axis_index("blk"), 2)
    total = own[...]
    held[chip] = own_terms[...].astype(F32)
    for k in range(1, half):
        total += parts[k - 1][:nodes].astype(F32)
        held[lax.bitwise_xor(chip, k)] = parts[k - 1][nodes:].astype(F32)
    grads[...] = total
    gw = held[0]
    for k in range(1, half):
        gw += held[k]
    terms[...] = gw


def join_cores(mine, arrived, out):
    core = lax.rem(lax.axis_index("blk"), 2)
    rows = mine.shape[0]
    out[pl.ds(pl.multiple_of(core * rows, rows), rows), :] = mine[...]
    out[pl.ds(pl.multiple_of((1 - core) * rows, rows), rows), :] = arrived[...]


def per_device(feats, weight, cotangent, block_vals, block_rows, block_cols, step_counts):
    reps = lax.axis_size("rep")
    groups = lax.axis_size("blk")
    lists, cap, block = block_vals.shape[2:5]
    nodes, width = feats.shape
    part = width // reps
    slots = lists * cap
    half = groups // 2
    like = jax.ShapeDtypeStruct

    def direct(arrays):
        return [arrays[0]] + [swap(arrays[x], "rep", x) for x in range(1, reps)]

    adjacency = block_vals.reshape(slots, block, block)
    evens = spread(adjacency, 2)
    odds = [swap(adjacency, "rep", 1)]
    chunks = call(
        functools.partial(split_features, reps, lists, cap),
        [like((part + PAD, nodes), BF16)] * reps,
        [VMEM, SMEM, SMEM, SMEM],
        [pltpu.VMEM((reps, part, nodes), BF16)],
        moved=4 * nodes * width,
    )(feats, block_rows[0, 0], block_cols[0, 0], step_counts[0, 0])
    mine, index, cotangent, *relayed = call(
        functools.partial(order_chunks, reps, part),
        [like((reps, part, nodes), BF16), like((reps, PAD, nodes), jnp.int32)]
        + [like((nodes, width), BF16)]
        + [like((slots, block, block), BF16)] * (reps // 2 - 1),
        [VMEM] * (reps + reps // 2) + [pl.BlockSpec(memory_space=pl.ANY)],
        moved=4 * nodes * width,
    )(*direct(chunks), cotangent, *evens[1:], odds[0])
    odds += [swap(array, "rep", 1) for array in relayed]
    blocks = [array for pair in zip(evens, odds) for array in pair]

    near, cotangents = call(
        functools.partial(join, half),
        [like((half, reps, part, nodes), BF16), like((reps // 2, nodes, width), BF16)],
        [VMEM] * (half + reps // 2) + [pl.BlockSpec(memory_space=pl.ANY)] * (reps // 2 - 1),
        moved=4 * half * nodes * width,
    )(
        mine,
        *[swap(mine, "blk", 2 * k) for k in range(1, half)],
        *spread(cotangent, 2),
        *odds[1:],
    )
    far = swap(near, "blk", 1)
    slot_flops = 2 * groups * cap * part * block * block
    slot_bytes = 2 * (groups * cap * block * block + groups * nodes * width)

    agg = call(
        functools.partial(aggregate, reps, groups, lists, cap),
        like((reps, part, nodes), BF16),
        [SMEM] + [VMEM] * (reps + 2),
        [pltpu.VMEM((reps, part, nodes), F32)],
        flops=slot_flops,
        moved=slot_bytes,
    )(index, *blocks, near, far)

    out_rows, dagg, terms = call(
        functools.partial(dense_layer, reps),
        [
            like((nodes, width), BF16),
            like((reps, nodes, width), BF16),
            like((2, width // 2, width), BF16),
        ],
        [VMEM] * (reps + 3),
        [
            pltpu.VMEM((reps, reps, part, nodes), BF16),
            pltpu.VMEM((reps, nodes, width), BF16),
            pltpu.VMEM((reps, nodes, width), BF16),
        ],
        flops=6 * reps * nodes * width * width,
        moved=2 * reps * 5 * nodes * width,
    )(*direct([agg] * reps), cotangents, swap(cotangents, "rep", 1), weight)

    keep, send = call(
        functools.partial(feature_grads, reps, groups, lists, cap),
        [
            like((half, nodes, width), F32),
            like((half + width // 2 // nodes, nodes, width), BF16),
        ],
        [SMEM] + [VMEM] * (reps + 2),
        [pltpu.VMEM((half, nodes, width), F32)],
        flops=slot_flops,
        moved=slot_bytes,
    )(index, *blocks, dagg, terms)
    own, own_terms, *sends = call(
        functools.partial(add_core, half),
        [like((nodes, width), F32), like((width // 2, width), BF16)]
        + [like((nodes + width // 2, width), BF16)] * (half - 1),
        [VMEM] * 3,
        moved=10 * half * nodes * width,
    )(keep, terms, swap(send, "blk", 1))
    grad_feats, terms = call(
        functools.partial(add_chips, half),
        [like((nodes, width), F32), like((width // 2, width), F32)],
        [VMEM] * (half + 1),
        [pltpu.VMEM((half, width // 2, width), F32)],
        moved=8 * half * nodes * width,
    )(own, own_terms, *[swap(sends[k - 1], "blk", 2 * k) for k in range(1, half)])
    grad_weight = call(
        join_cores, like((width, width), F32), [VMEM] * 2, moved=8 * width * width
    )(terms, swap(terms, "blk", 1))
    return (out_rows, grad_weight, grad_feats)


def solution(mesh):
    return jax.shard_map(
        per_device,
        mesh=mesh,
        in_specs=(
            P(("blk", "rep"), None),
            P(),
            P(("blk", "rep"), None),
            P("blk", "rep", None, None, None, None),
            P("blk", "rep", None, None),
            P("blk", "rep", None, None),
            P("blk", "rep", None),
        ),
        out_specs=(P(("blk", "rep"), None), P(), P(("blk", "rep"), None)),
        check_vma=False,
    )
```

```python
import functools

import jax
import jax.numpy as jnp
from jax import lax
from jax.experimental import pallas as pl
from jax.experimental.pallas import tpu as pltpu
from jax.sharding import PartitionSpec as P

F32 = jnp.float32
BF16 = jnp.bfloat16
VMEM = pl.BlockSpec(memory_space=pltpu.VMEM)
SMEM = pl.BlockSpec(memory_space=pltpu.SMEM)
PAD = 16


def swap(array, axis, bit):
    peers = lax.axis_size(axis)
    return lax.ppermute(array, axis, [(i, i ^ bit) for i in range(peers)])


def spread(array, last=1):
    reps = lax.axis_size("rep")
    held = {0: array}
    bit = reps // 2
    while bit >= last:
        held.update({x | bit: swap(part, "rep", bit) for x, part in held.items()})
        bit //= 2
    return [held[x] for x in sorted(held)]


def call(body, outs, in_specs, scratch=(), flops=0, moved=0):
    return pl.pallas_call(
        body,
        out_shape=outs,
        in_specs=in_specs,
        out_specs=jax.tree.map(lambda _: VMEM, outs),
        scratch_shapes=list(scratch),
        compiler_params=pltpu.CompilerParams(vmem_limit_bytes=48 * 1024 * 1024),
        cost_estimate=pl.CostEstimate(flops=flops, bytes_accessed=moved, transcendentals=0),
    )


def dot(a, b, a_dim, b_dim):
    return lax.dot_general(a, b, (((a_dim,), (b_dim,)), ((), ())), preferred_element_type=F32)


def other(axis, by):
    return lax.bitwise_xor(lax.axis_index(axis), by)


def split_features(reps, lists, cap, feats, rows, cols, counts, *rest):
    outs, turned = rest[:-1], rest[-1]
    nodes = feats.shape[0]
    part = feats.shape[1] // reps
    turned[...] = feats[...].astype(F32).T.astype(BF16).reshape(turned.shape)
    lane = lax.broadcasted_iota(jnp.int32, (PAD, nodes), 1)
    index = jnp.zeros((PAD, nodes), jnp.int32)
    slots = lists * cap
    for j in range(lists):
        for c in range(cap):
            k = j * cap + c
            index = jnp.where(lane == k, rows[j, c], index)
            index = jnp.where(lane == slots + k, cols[j, c], index)
        index = jnp.where(lane == 2 * slots + j, counts[j], index)
    index = index.astype(F32).astype(BF16)
    for x in range(reps):
        outs[x][:part] = turned[other("rep", x)]
        outs[x][part:] = index


def order_chunks(reps, part, *refs):
    copies = reps // 2 - 1
    chunks, sources, unread = refs[:reps], refs[reps : reps + copies], refs[reps + copies]
    mine, index = refs[reps + copies + 1 : reps + copies + 3]
    for source, target in zip(sources, refs[reps + copies + 3 :]):
        target[...] = source[...]
    for x in range(reps):
        mine[other("rep", x)] = chunks[x][:part]
        index[x] = chunks[x][part:].astype(F32).astype(jnp.int32)[:1]


def join(half, *refs):
    out, pairs = refs[-2:]
    for k, ref in enumerate(refs[:half]):
        out[k] = ref[...]
    for k in range(pairs.shape[0]):
        pairs[k] = refs[half + k][...]


def slot_of(index, lists, cap, t, j, c):
    k = j * cap + c
    slots = lists * cap
    return index[t, 0, k], index[t, 0, slots + k], c < index[t, 0, 2 * slots + j]


def relative(groups, lists, x, j):
    mine = lax.axis_index("blk")
    offset = other("rep", x) * lists + j
    return lax.div(lax.bitwise_xor(mine, lax.rem(mine + groups - offset, groups)), 2)


def aggregate(reps, groups, lists, cap, parity, index, *refs):
    blocks, held, start, out = refs[:reps], refs[reps], refs[reps + 1 : -2], refs[-2]
    total = refs[-1]
    total[...] = start[0][...] if start else jnp.zeros_like(total)
    for x in range(reps):
        for j in range(parity, lists, 2):
            place = relative(groups, lists, x, j)
            for c in range(cap):
                row, col, live = slot_of(index, lists, cap, x, j, c)
                product = dot(held[place, col], blocks[x][j * cap + c], 1, 1)
                total[row] += jnp.where(live, product, 0.0)
    out[...] = total[...].astype(out.dtype)


def dense_layer(reps, *refs):
    chunks = refs[:reps]
    cotangents = refs[reps : reps + 2]
    weight, out, dagg, terms, agg, cot, outs = refs[reps + 2 :]
    nodes, width = out.shape
    for x in range(reps):
        origin = other("rep", x)
        cot[origin] = cotangents[x % 2][x // 2]
        for b in range(reps):
            agg[b, origin] = chunks[x][b]
    gw = jnp.zeros((width, width), F32)
    for b in range(reps):
        turned = agg[b].reshape(width, nodes)
        pre = dot(turned, weight[...], 0, 0)
        sigma = jax.nn.sigmoid(pre)
        outs[b] = (pre * sigma).astype(BF16)
        slope = sigma * (1.0 + pre * (1.0 - sigma))
        dpre = (cot[b].astype(F32) * slope).astype(BF16)
        dagg[b] = dot(dpre, weight[...], 1, 1).astype(BF16)
        gw += dot(turned, dpre, 1, 0)
    out[...] = outs[lax.axis_index("rep")]
    terms[...] = gw.astype(BF16).reshape(terms.shape)


def feature_grads(reps, groups, lists, cap, index, *refs):
    blocks = refs[:reps]
    dagg, terms, keep, send, total = refs[reps:]
    me = lax.axis_index("rep")
    half = groups // 2
    keep[...] = jnp.zeros_like(keep)
    total[...] = jnp.zeros_like(total)
    for x in range(reps):
        for j in range(lists):
            target = total if j % 2 else keep
            place = relative(groups, lists, x, j)
            for c in range(cap):
                row, col, live = slot_of(index, lists, cap, x, j, c)

                @pl.when(jnp.logical_and(live, col == me))
                def _():
                    target[place] += dot(blocks[x][j * cap + c], dagg[row], 0, 0)

    send[:half] = total[...].astype(BF16)
    core = lax.rem(lax.axis_index("blk"), 2)
    send[half:] = terms[1 - core].reshape(-1, *send.shape[1:])


def add_core(half, keep, terms, arrived, own, own_terms, *sends):
    nodes = own.shape[0]
    own[...] = keep[0] + arrived[0].astype(F32)
    core = lax.rem(lax.axis_index("blk"), 2)
    mine = terms[core].astype(F32)
    gw = (mine + arrived[half:].reshape(mine.shape).astype(F32)).astype(BF16)
    own_terms[...] = gw
    for k in range(1, half):
        sends[k - 1][:nodes] = (keep[k] + arrived[k].astype(F32)).astype(BF16)
        sends[k - 1][nodes:] = gw


def add_chips(half, own, own_terms, *refs):
    parts, grads, terms, held = refs[: half - 1], refs[-3], refs[-2], refs[-1]
    nodes = own.shape[0]
    chip = lax.div(lax.axis_index("blk"), 2)
    total = own[...]
    held[chip] = own_terms[...].astype(F32)
    for k in range(1, half):
        total += parts[k - 1][:nodes].astype(F32)
        held[lax.bitwise_xor(chip, k)] = parts[k - 1][nodes:].astype(F32)
    grads[...] = total
    gw = held[0]
    for k in range(1, half):
        gw += held[k]
    terms[...] = gw


def store(grads, rows, grad_feats, out_rows):
    grad_feats[...] = grads[...]
    out_rows[...] = rows[...]


def join_cores(mine, arrived, out):
    core = lax.rem(lax.axis_index("blk"), 2)
    rows = mine.shape[0]
    out[pl.ds(pl.multiple_of(core * rows, rows), rows), :] = mine[...]
    out[pl.ds(pl.multiple_of((1 - core) * rows, rows), rows), :] = arrived[...]


def per_device(feats, weight, cotangent, block_vals, block_rows, block_cols, step_counts):
    reps = lax.axis_size("rep")
    groups = lax.axis_size("blk")
    lists, cap, block = block_vals.shape[2:5]
    nodes, width = feats.shape
    part = width // reps
    slots = lists * cap
    half = groups // 2
    like = jax.ShapeDtypeStruct

    def direct(arrays):
        return [arrays[0]] + [swap(arrays[x], "rep", x) for x in range(1, reps)]

    adjacency = block_vals.reshape(slots, block, block)
    evens = spread(adjacency, 2)
    odds = [swap(adjacency, "rep", 1)]
    chunks = call(
        functools.partial(split_features, reps, lists, cap),
        [like((part + PAD, nodes), BF16)] * reps,
        [VMEM, SMEM, SMEM, SMEM],
        [pltpu.VMEM((reps, part, nodes), BF16)],
        moved=4 * nodes * width,
    )(feats, block_rows[0, 0], block_cols[0, 0], step_counts[0, 0])
    mine, index, *relayed = call(
        functools.partial(order_chunks, reps, part),
        [like((reps, part, nodes), BF16), like((reps, 1, nodes), jnp.int32)]
        + [like((slots, block, block), BF16)] * (reps // 2 - 1),
        [VMEM] * (reps + reps // 2 - 1) + [pl.BlockSpec(memory_space=pl.ANY)],
        moved=4 * nodes * width,
    )(*direct(chunks), *evens[1:], odds[0])
    odds += [swap(array, "rep", 1) for array in relayed]
    blocks = [array for pair in zip(evens, odds) for array in pair]

    near, cotangents = call(
        functools.partial(join, half),
        [like((half, reps, part, nodes), BF16), like((reps // 2, nodes, width), BF16)],
        [VMEM] * (half + reps // 2) + [pl.BlockSpec(memory_space=pl.ANY)] * (reps // 2 - 1),
        moved=4 * half * nodes * width,
    )(
        mine,
        *[swap(mine, "blk", 2 * k) for k in range(1, half)],
        *spread(cotangent, 2),
        *odds[1:],
    )
    far = swap(near, "blk", 1)
    slot_flops = 2 * groups * cap * part * block * block
    slot_bytes = 2 * (groups * cap * block * block + groups * nodes * width)

    agg = call(
        functools.partial(aggregate, reps, groups, lists, cap, 0),
        like((reps, part, nodes), F32),
        [SMEM] + [VMEM] * (reps + 1),
        [pltpu.VMEM((reps, part, nodes), F32)],
        flops=slot_flops // 2,
        moved=slot_bytes // 2,
    )(index, *blocks, near)
    agg = call(
        functools.partial(aggregate, reps, groups, lists, cap, 1),
        like((reps, part, nodes), BF16),
        [SMEM] + [VMEM] * (reps + 2),
        [pltpu.VMEM((reps, part, nodes), F32)],
        flops=slot_flops // 2,
        moved=slot_bytes // 2,
    )(index, *blocks, far, agg)

    out_rows, dagg, terms = call(
        functools.partial(dense_layer, reps),
        [
            like((nodes, width), BF16),
            like((reps, nodes, width), BF16),
            like((2, width // 2, width), BF16),
        ],
        [VMEM] * (reps + 3),
        [
            pltpu.VMEM((reps, reps, part, nodes), BF16),
            pltpu.VMEM((reps, nodes, width), BF16),
            pltpu.VMEM((reps, nodes, width), BF16),
        ],
        flops=6 * reps * nodes * width * width,
        moved=2 * reps * 5 * nodes * width,
    )(*direct([agg] * reps), cotangents, swap(cotangents, "rep", 1), weight)

    keep, send = call(
        functools.partial(feature_grads, reps, groups, lists, cap),
        [
            like((half, nodes, width), F32),
            like((half + width // 2 // nodes, nodes, width), BF16),
        ],
        [SMEM] + [VMEM] * (reps + 2),
        [pltpu.VMEM((half, nodes, width), F32)],
        flops=slot_flops,
        moved=slot_bytes,
    )(index, *blocks, dagg, terms)
    own, own_terms, *sends = call(
        functools.partial(add_core, half),
        [like((nodes, width), F32), like((width // 2, width), BF16)]
        + [like((nodes + width // 2, width), BF16)] * (half - 1),
        [VMEM] * 3,
        moved=10 * half * nodes * width,
    )(keep, terms, swap(send, "blk", 1))
    grads, terms = call(
        functools.partial(add_chips, half),
        [like((nodes, width), F32), like((width // 2, width), F32)],
        [VMEM] * (half + 1),
        [pltpu.VMEM((half, width // 2, width), F32)],
        moved=8 * half * nodes * width,
    )(own, own_terms, *[swap(sends[k - 1], "blk", 2 * k) for k in range(1, half)])
    grad_feats, out_rows = call(
        store,
        [like((nodes, width), F32), like((nodes, width), BF16)],
        [VMEM] * 2,
        moved=12 * nodes * width,
    )(grads, out_rows)
    grad_weight = call(
        join_cores, like((width, width), F32), [VMEM] * 2, moved=8 * width * width
    )(terms, swap(terms, "blk", 1))
    return (out_rows, grad_weight, grad_feats)


def solution(mesh):
    return jax.shard_map(
        per_device,
        mesh=mesh,
        in_specs=(
            P(("blk", "rep"), None),
            P(),
            P(("blk", "rep"), None),
            P("blk", "rep", None, None, None, None),
            P("blk", "rep", None, None),
            P("blk", "rep", None, None),
            P("blk", "rep", None),
        ),
        out_specs=(P(("blk", "rep"), None), P(), P(("blk", "rep"), None)),
        check_vma=False,
    )
```

```python
import functools

import jax
import jax.numpy as jnp
from jax import lax
from jax.experimental import pallas as pl
from jax.experimental.pallas import tpu as pltpu
from jax.sharding import PartitionSpec as P

F32 = jnp.float32
BF16 = jnp.bfloat16
VMEM = pl.BlockSpec(memory_space=pltpu.VMEM)
SMEM = pl.BlockSpec(memory_space=pltpu.SMEM)
PAD = 16


def swap(array, axis, bit):
    peers = lax.axis_size(axis)
    return lax.ppermute(array, axis, [(i, i ^ bit) for i in range(peers)])


def spread(array, last=1):
    reps = lax.axis_size("rep")
    held = {0: array}
    bit = reps // 2
    while bit >= last:
        held.update({x | bit: swap(part, "rep", bit) for x, part in held.items()})
        bit //= 2
    return [held[x] for x in sorted(held)]


def call(body, outs, in_specs, scratch=(), flops=0, moved=0):
    return pl.pallas_call(
        body,
        out_shape=outs,
        in_specs=in_specs,
        out_specs=jax.tree.map(lambda _: VMEM, outs),
        scratch_shapes=list(scratch),
        compiler_params=pltpu.CompilerParams(vmem_limit_bytes=48 * 1024 * 1024),
        cost_estimate=pl.CostEstimate(flops=flops, bytes_accessed=moved, transcendentals=0),
    )


def dot(a, b, a_dim, b_dim):
    return lax.dot_general(a, b, (((a_dim,), (b_dim,)), ((), ())), preferred_element_type=F32)


def other(axis, by):
    return lax.bitwise_xor(lax.axis_index(axis), by)


def split_features(reps, lists, cap, feats, rows, cols, counts, *rest):
    outs, turned = rest[:-1], rest[-1]
    nodes = feats.shape[0]
    part = feats.shape[1] // reps
    turned[...] = feats[...].astype(F32).T.astype(BF16).reshape(turned.shape)
    lane = lax.broadcasted_iota(jnp.int32, (PAD, nodes), 1)
    index = jnp.zeros((PAD, nodes), jnp.int32)
    slots = lists * cap
    for j in range(lists):
        for c in range(cap):
            k = j * cap + c
            index = jnp.where(lane == k, rows[j, c], index)
            index = jnp.where(lane == slots + k, cols[j, c], index)
        index = jnp.where(lane == 2 * slots + j, counts[j], index)
    index = index.astype(F32).astype(BF16)
    for x in range(reps):
        outs[x][:part] = turned[other("rep", x)]
        outs[x][part:] = index


def order_chunks(reps, part, *refs):
    chunks, blocks, mine, index, later = refs[:reps], refs[reps], *refs[-3:]
    for x in range(reps):
        mine[other("rep", x)] = chunks[x][:part]
        index[x] = chunks[x][part:].astype(F32).astype(jnp.int32)[:1]
    later[...] = blocks[later.shape[0] :]


def stack(first, second, out):
    count = first.shape[0]
    out[:count] = first[...]
    out[count:] = second[...]


def join(half, *refs):
    out, pairs = refs[-2:]
    for k, ref in enumerate(refs[:half]):
        out[k] = ref[...]
    for k in range(pairs.shape[0]):
        pairs[k] = refs[half + k][...]


def slot_of(index, lists, cap, t, j, c):
    k = j * cap + c
    slots = lists * cap
    return index[t, 0, k], index[t, 0, slots + k], c < index[t, 0, 2 * slots + j]


def relative(groups, lists, x, j):
    mine = lax.axis_index("blk")
    offset = other("rep", x) * lists + j
    return lax.div(lax.bitwise_xor(mine, lax.rem(mine + groups - offset, groups)), 2)


def aggregate(reps, groups, lists, cap, first, index, *refs):
    known = reps - 1 if first else reps
    blocks, near, far = refs[:known], refs[known], refs[-4]
    start, out, total = refs[-3], refs[-2], refs[-1]
    total[...] = jnp.zeros_like(total) if first else start[...]
    for x in range(known):
        for j in range(lists):
            if first != (j % 2 == 0 and x < reps - 1):
                continue
            held = far if j % 2 else near
            place = relative(groups, lists, x, j)
            for c in range(cap):
                row, col, live = slot_of(index, lists, cap, x, j, c)
                product = dot(held[place, col], blocks[x][j * cap + c], 1, 1)
                total[row] += jnp.where(live, product, 0.0)
    out[...] = total[...].astype(out.dtype)


def dense_layer(reps, *refs):
    chunks = refs[:reps]
    cotangents = refs[reps : reps + 2]
    weight, out, dagg, terms, agg, cot, outs = refs[reps + 2 :]
    nodes, width = out.shape
    for x in range(reps):
        origin = other("rep", x)
        cot[origin] = cotangents[x % 2][x // 2]
        for b in range(reps):
            agg[b, origin] = chunks[x][b]
    gw = jnp.zeros((width, width), F32)
    for b in range(reps):
        turned = agg[b].reshape(width, nodes)
        pre = dot(turned, weight[...], 0, 0)
        sigma = jax.nn.sigmoid(pre)
        outs[b] = (pre * sigma).astype(BF16)
        slope = sigma * (1.0 + pre * (1.0 - sigma))
        dpre = (cot[b].astype(F32) * slope).astype(BF16)
        dagg[b] = dot(dpre, weight[...], 1, 1).astype(BF16)
        gw += dot(turned, dpre, 1, 0)
    out[...] = outs[lax.axis_index("rep")]
    terms[...] = gw.astype(BF16).reshape(terms.shape)


def feature_grads(reps, groups, lists, cap, parity, index, *refs):
    blocks, dagg, rest = refs[:reps], refs[reps], refs[reps + 1 :]
    me = lax.axis_index("rep")
    half = groups // 2
    total = rest[-1]
    total[...] = jnp.zeros_like(total)
    for x in range(reps):
        for j in range(parity, lists, 2):
            place = relative(groups, lists, x, j)
            for c in range(cap):
                row, col, live = slot_of(index, lists, cap, x, j, c)

                @pl.when(jnp.logical_and(live, col == me))
                def _():
                    total[place] += dot(blocks[x][j * cap + c], dagg[row], 0, 0)

    if parity:
        terms, send = rest[:2]
        send[:half] = total[...].astype(BF16)
        core = lax.rem(lax.axis_index("blk"), 2)
        send[half:] = terms[1 - core].reshape(-1, *send.shape[1:])


def add_core(half, keep, terms, arrived, own, own_terms, *sends):
    nodes = own.shape[0]
    own[...] = keep[0] + arrived[0].astype(F32)
    core = lax.rem(lax.axis_index("blk"), 2)
    mine = terms[core].astype(F32)
    gw = (mine + arrived[half:].reshape(mine.shape).astype(F32)).astype(BF16)
    own_terms[...] = gw
    for k in range(1, half):
        sends[k - 1][:nodes] = (keep[k] + arrived[k].astype(F32)).astype(BF16)
        sends[k - 1][nodes:] = gw


def add_chips(half, own, own_terms, *refs):
    parts, grads, terms, held = refs[: half - 1], refs[-3], refs[-2], refs[-1]
    nodes = own.shape[0]
    chip = lax.div(lax.axis_index("blk"), 2)
    total = own[...]
    held[chip] = own_terms[...].astype(F32)
    for k in range(1, half):
        total += parts[k - 1][:nodes].astype(F32)
        held[lax.bitwise_xor(chip, k)] = parts[k - 1][nodes:].astype(F32)
    grads[...] = total
    gw = held[0]
    for k in range(1, half):
        gw += held[k]
    terms[...] = gw


def store(grads, rows, grad_feats, out_rows):
    grad_feats[...] = grads[...]
    out_rows[...] = rows[...]


def join_cores(mine, arrived, out):
    core = lax.rem(lax.axis_index("blk"), 2)
    rows = mine.shape[0]
    out[pl.ds(pl.multiple_of(core * rows, rows), rows), :] = mine[...]
    out[pl.ds(pl.multiple_of((1 - core) * rows, rows), rows), :] = arrived[...]


def per_device(feats, weight, cotangent, block_vals, block_rows, block_cols, step_counts):
    reps = lax.axis_size("rep")
    groups = lax.axis_size("blk")
    lists, cap, block = block_vals.shape[2:5]
    nodes, width = feats.shape
    part = width // reps
    slots = lists * cap
    half = groups // 2
    like = jax.ShapeDtypeStruct

    def direct(arrays):
        return [arrays[0]] + [swap(arrays[x], "rep", x) for x in range(1, reps)]

    unread = pl.BlockSpec(memory_space=pl.ANY)
    adjacency = block_vals.reshape(slots, block, block)
    odds = [swap(adjacency, "rep", 1)]
    early = spread(adjacency[: slots // 2], 2)[1:]
    chunks = call(
        functools.partial(split_features, reps, lists, cap),
        [like((part + PAD, nodes), BF16)] * reps,
        [VMEM, SMEM, SMEM, SMEM],
        [pltpu.VMEM((reps, part, nodes), BF16)],
        moved=4 * nodes * width,
    )(feats, block_rows[0, 0], block_cols[0, 0], step_counts[0, 0])
    mine, index, later = call(
        functools.partial(order_chunks, reps, part),
        [
            like((reps, part, nodes), BF16),
            like((reps, 1, nodes), jnp.int32),
            like((slots - slots // 2, block, block), BF16),
        ],
        [VMEM] * (reps + 1) + [unread] * (reps // 2),
        moved=4 * nodes * width,
    )(*direct(chunks), adjacency, *odds, *early)
    evens = [
        call(stack, like(adjacency.shape, BF16), [VMEM] * 2, moved=4 * adjacency.size)(one, two)
        for one, two in zip(early, spread(later, 2)[1:])
    ]
    odds += [swap(array, "rep", 1) for array in evens]
    blocks = [array for pair in zip([adjacency] + evens, odds) for array in pair]

    near, cotangents = call(
        functools.partial(join, half),
        [like((half, reps, part, nodes), BF16), like((reps // 2, nodes, width), BF16)],
        [VMEM] * (half + reps // 2) + [unread] * (reps // 2 - 1),
        moved=4 * half * nodes * width,
    )(
        mine,
        *[swap(mine, "blk", 2 * k) for k in range(1, half)],
        *spread(cotangent, 2),
        *evens,
    )
    far = swap(near, "blk", 1)
    slot_flops = 2 * groups * cap * part * block * block
    slot_bytes = 2 * (groups * cap * block * block + groups * nodes * width)

    agg = call(
        functools.partial(aggregate, reps, groups, lists, cap, True),
        like((reps, part, nodes), F32),
        [SMEM] + [VMEM] * reps,
        [pltpu.VMEM((reps, part, nodes), F32)],
        flops=slot_flops // 2,
        moved=slot_bytes // 2,
    )(index, *blocks[:-1], near)
    agg = call(
        functools.partial(aggregate, reps, groups, lists, cap, False),
        like((reps, part, nodes), BF16),
        [SMEM] + [VMEM] * (reps + 3),
        [pltpu.VMEM((reps, part, nodes), F32)],
        flops=slot_flops // 2,
        moved=slot_bytes // 2,
    )(index, *blocks, near, far, agg)
    aggs = direct([agg] * reps)

    out_rows, dagg, terms = call(
        functools.partial(dense_layer, reps),
        [
            like((nodes, width), BF16),
            like((reps, nodes, width), BF16),
            like((2, width // 2, width), BF16),
        ],
        [VMEM] * (reps + 3),
        [
            pltpu.VMEM((reps, reps, part, nodes), BF16),
            pltpu.VMEM((reps, nodes, width), BF16),
            pltpu.VMEM((reps, nodes, width), BF16),
        ],
        flops=6 * reps * nodes * width * width,
        moved=2 * reps * 5 * nodes * width,
    )(*aggs, cotangents, swap(cotangents, "rep", 1), weight)

    send = call(
        functools.partial(feature_grads, reps, groups, lists, cap, 1),
        like((half + width // 2 // nodes, nodes, width), BF16),
        [SMEM] + [VMEM] * (reps + 2),
        [pltpu.VMEM((half, nodes, width), F32)],
        flops=slot_flops // 2,
        moved=slot_bytes // 2,
    )(index, *blocks, dagg, terms)
    keep = call(
        functools.partial(feature_grads, reps, groups, lists, cap, 0),
        like((half, nodes, width), F32),
        [SMEM] + [VMEM] * (reps + 1),
        flops=slot_flops // 2,
        moved=slot_bytes // 2,
    )(index, *blocks, dagg)
    own, own_terms, *sends = call(
        functools.partial(add_core, half),
        [like((nodes, width), F32), like((width // 2, width), BF16)]
        + [like((nodes + width // 2, width), BF16)] * (half - 1),
        [VMEM] * 3,
        moved=10 * half * nodes * width,
    )(keep, terms, swap(send, "blk", 1))
    grads, terms = call(
        functools.partial(add_chips, half),
        [like((nodes, width), F32), like((width // 2, width), F32)],
        [VMEM] * (half + 1),
        [pltpu.VMEM((half, width // 2, width), F32)],
        moved=8 * half * nodes * width,
    )(own, own_terms, *[swap(sends[k - 1], "blk", 2 * k) for k in range(1, half)])
    grad_feats, out_rows = call(
        store,
        [like((nodes, width), F32), like((nodes, width), BF16)],
        [VMEM] * 2,
        moved=12 * nodes * width,
    )(grads, out_rows)
    grad_weight = call(
        join_cores, like((width, width), F32), [VMEM] * 2, moved=8 * width * width
    )(terms, swap(terms, "blk", 1))
    return (out_rows, grad_weight, grad_feats)


def solution(mesh):
    return jax.shard_map(
        per_device,
        mesh=mesh,
        in_specs=(
            P(("blk", "rep"), None),
            P(),
            P(("blk", "rep"), None),
            P("blk", "rep", None, None, None, None),
            P("blk", "rep", None, None),
            P("blk", "rep", None, None),
            P("blk", "rep", None),
        ),
        out_specs=(P(("blk", "rep"), None), P(), P(("blk", "rep"), None)),
        check_vma=False,
    )
```

```python
import functools

import jax
import jax.numpy as jnp
from jax import lax
from jax.experimental import pallas as pl
from jax.experimental.pallas import tpu as pltpu
from jax.sharding import PartitionSpec as P

F32 = jnp.float32
BF16 = jnp.bfloat16
VMEM = pl.BlockSpec(memory_space=pltpu.VMEM)
SMEM = pl.BlockSpec(memory_space=pltpu.SMEM)
PAD = 16


def swap(array, axis, bit):
    peers = lax.axis_size(axis)
    return lax.ppermute(array, axis, [(i, i ^ bit) for i in range(peers)])


def spread(array, last=1):
    reps = lax.axis_size("rep")
    held = {0: array}
    bit = reps // 2
    while bit >= last:
        held.update({x | bit: swap(part, "rep", bit) for x, part in held.items()})
        bit //= 2
    return [held[x] for x in sorted(held)]


def call(body, outs, in_specs, scratch=(), flops=0, moved=0):
    return pl.pallas_call(
        body,
        out_shape=outs,
        in_specs=in_specs,
        out_specs=jax.tree.map(lambda _: VMEM, outs),
        scratch_shapes=list(scratch),
        compiler_params=pltpu.CompilerParams(vmem_limit_bytes=48 * 1024 * 1024),
        cost_estimate=pl.CostEstimate(flops=flops, bytes_accessed=moved, transcendentals=0),
    )


def dot(a, b, a_dim, b_dim):
    return lax.dot_general(a, b, (((a_dim,), (b_dim,)), ((), ())), preferred_element_type=F32)


def other(axis, by):
    return lax.bitwise_xor(lax.axis_index(axis), by)


def split_features(reps, lists, cap, feats, rows, cols, counts, *rest):
    outs, turned = rest[:-1], rest[-1]
    nodes = feats.shape[0]
    part = feats.shape[1] // reps
    turned[...] = feats[...].astype(F32).T.astype(BF16).reshape(turned.shape)
    lane = lax.broadcasted_iota(jnp.int32, (PAD, nodes), 1)
    index = jnp.zeros((PAD, nodes), jnp.int32)
    slots = lists * cap
    for j in range(lists):
        for c in range(cap):
            k = j * cap + c
            index = jnp.where(lane == k, rows[j, c], index)
            index = jnp.where(lane == slots + k, cols[j, c], index)
        index = jnp.where(lane == 2 * slots + j, counts[j], index)
    index = index.astype(F32).astype(BF16)
    for x in range(reps):
        outs[x][:part] = turned[other("rep", x)]
        outs[x][part:] = index


def order_chunks(reps, part, *refs):
    copies = reps // 2 - 1
    chunks, sources, unread = refs[:reps], refs[reps : reps + copies], refs[reps + copies]
    mine, index = refs[reps + copies + 1 : reps + copies + 3]
    for source, target in zip(sources, refs[reps + copies + 3 :]):
        target[...] = source[...]
    for x in range(reps):
        mine[other("rep", x)] = chunks[x][:part]
        index[x] = chunks[x][part:].astype(F32).astype(jnp.int32)[:1]


def join(half, *refs):
    out, pairs = refs[-2:]
    for k, ref in enumerate(refs[:half]):
        out[k] = ref[...]
    for k in range(pairs.shape[0]):
        pairs[k] = refs[half + k][...]


def slot_of(index, lists, cap, t, j, c):
    k = j * cap + c
    slots = lists * cap
    return index[t, 0, k], index[t, 0, slots + k], c < index[t, 0, 2 * slots + j]


def relative(groups, lists, x, j):
    mine = lax.axis_index("blk")
    offset = other("rep", x) * lists + j
    return lax.div(lax.bitwise_xor(mine, lax.rem(mine + groups - offset, groups)), 2)


def aggregate(reps, groups, lists, cap, parity, index, *refs):
    blocks, held, start, out = refs[:reps], refs[reps], refs[reps + 1 : -2], refs[-2]
    total = refs[-1]
    total[...] = start[0][...] if start else jnp.zeros_like(total)
    for x in range(reps):
        for j in range(parity, lists, 2):
            place = relative(groups, lists, x, j)
            for c in range(cap):
                row, col, live = slot_of(index, lists, cap, x, j, c)
                product = dot(held[place, col], blocks[x][j * cap + c], 1, 1)
                total[row] += jnp.where(live, product, 0.0)
    out[...] = total[...].astype(out.dtype)


def dense_layer(reps, *refs):
    chunks = refs[:reps]
    cotangents = refs[reps : reps + 2]
    weight, out, dagg, terms, agg, cot, outs = refs[reps + 2 :]
    nodes, width = out.shape
    for x in range(reps):
        origin = other("rep", x)
        cot[origin] = cotangents[x % 2][x // 2]
        for b in range(reps):
            agg[b, origin] = chunks[x][b]
    gw = jnp.zeros((width, width), F32)
    for b in range(reps):
        turned = agg[b].reshape(width, nodes)
        pre = dot(turned, weight[...], 0, 0)
        sigma = jax.nn.sigmoid(pre)
        outs[b] = (pre * sigma).astype(BF16)
        slope = sigma * (1.0 + pre * (1.0 - sigma))
        dpre = (cot[b].astype(F32) * slope).astype(BF16)
        dagg[b] = dot(dpre, weight[...], 1, 1).astype(BF16)
        gw += dot(turned, dpre, 1, 0)
    out[...] = outs[lax.axis_index("rep")]
    terms[...] = gw.astype(BF16).reshape(terms.shape)


def feature_grads(reps, groups, lists, cap, parity, index, *refs):
    blocks, dagg, rest = refs[:reps], refs[reps], refs[reps + 1 :]
    me = lax.axis_index("rep")
    half = groups // 2
    total = rest[-1]
    total[...] = jnp.zeros_like(total)
    for x in range(reps):
        for j in range(parity, lists, 2):
            place = relative(groups, lists, x, j)
            for c in range(cap):
                row, col, live = slot_of(index, lists, cap, x, j, c)

                @pl.when(jnp.logical_and(live, col == me))
                def _():
                    total[place] += dot(blocks[x][j * cap + c], dagg[row], 0, 0)

    if parity:
        terms, send = rest[:2]
        send[:half] = total[...].astype(BF16)
        core = lax.rem(lax.axis_index("blk"), 2)
        send[half:] = terms[1 - core].reshape(-1, *send.shape[1:])


def add_core(half, keep, terms, arrived, own, own_terms, *sends):
    nodes = own.shape[0]
    own[...] = keep[0] + arrived[0].astype(F32)
    core = lax.rem(lax.axis_index("blk"), 2)
    mine = terms[core].astype(F32)
    gw = (mine + arrived[half:].reshape(mine.shape).astype(F32)).astype(BF16)
    own_terms[...] = gw
    for k in range(1, half):
        sends[half - 1 - k][:nodes] = (keep[k] + arrived[k].astype(F32)).astype(BF16)
        sends[half - 1 - k][nodes:] = gw


def add_chips(half, own, own_terms, *refs):
    parts, grads, terms, held = refs[: half - 1], refs[-3], refs[-2], refs[-1]
    nodes = own.shape[0]
    chip = lax.div(lax.axis_index("blk"), 2)
    total = own[...]
    held[chip] = own_terms[...].astype(F32)
    for k in range(1, half):
        total += parts[half - 1 - k][:nodes].astype(F32)
        held[lax.bitwise_xor(chip, k)] = parts[half - 1 - k][nodes:].astype(F32)
    grads[...] = total
    gw = held[0]
    for k in range(1, half):
        gw += held[k]
    terms[...] = gw


def store(grads, rows, grad_feats, out_rows):
    grad_feats[...] = grads[...]
    out_rows[...] = rows[...]


def join_cores(mine, arrived, out):
    core = lax.rem(lax.axis_index("blk"), 2)
    rows = mine.shape[0]
    out[pl.ds(pl.multiple_of(core * rows, rows), rows), :] = mine[...]
    out[pl.ds(pl.multiple_of((1 - core) * rows, rows), rows), :] = arrived[...]


def per_device(feats, weight, cotangent, block_vals, block_rows, block_cols, step_counts):
    reps = lax.axis_size("rep")
    groups = lax.axis_size("blk")
    lists, cap, block = block_vals.shape[2:5]
    nodes, width = feats.shape
    part = width // reps
    slots = lists * cap
    half = groups // 2
    like = jax.ShapeDtypeStruct

    def direct(arrays):
        return [arrays[0]] + [swap(arrays[x], "rep", x) for x in range(1, reps)]

    adjacency = block_vals.reshape(slots, block, block)
    evens = spread(adjacency, 2)
    odds = [swap(adjacency, "rep", 1)]
    chunks = call(
        functools.partial(split_features, reps, lists, cap),
        [like((part + PAD, nodes), BF16)] * reps,
        [VMEM, SMEM, SMEM, SMEM],
        [pltpu.VMEM((reps, part, nodes), BF16)],
        moved=4 * nodes * width,
    )(feats, block_rows[0, 0], block_cols[0, 0], step_counts[0, 0])
    mine, index, *relayed = call(
        functools.partial(order_chunks, reps, part),
        [like((reps, part, nodes), BF16), like((reps, 1, nodes), jnp.int32)]
        + [like((slots, block, block), BF16)] * (reps // 2 - 1),
        [VMEM] * (reps + reps // 2 - 1) + [pl.BlockSpec(memory_space=pl.ANY)],
        moved=4 * nodes * width,
    )(*direct(chunks), *evens[1:], odds[0])
    odds += [swap(array, "rep", 1) for array in relayed]
    blocks = [array for pair in zip(evens, odds) for array in pair]

    near, cotangents = call(
        functools.partial(join, half),
        [like((half, reps, part, nodes), BF16), like((reps // 2, nodes, width), BF16)],
        [VMEM] * (half + reps // 2) + [pl.BlockSpec(memory_space=pl.ANY)] * (reps // 2 - 1),
        moved=4 * half * nodes * width,
    )(
        mine,
        *[swap(mine, "blk", 2 * k) for k in range(1, half)],
        *spread(cotangent, 2),
        *odds[1:],
    )
    far = swap(near, "blk", 1)
    slot_flops = 2 * groups * cap * part * block * block
    slot_bytes = 2 * (groups * cap * block * block + groups * nodes * width)

    agg = call(
        functools.partial(aggregate, reps, groups, lists, cap, 0),
        like((reps, part, nodes), F32),
        [SMEM] + [VMEM] * (reps + 1),
        [pltpu.VMEM((reps, part, nodes), F32)],
        flops=slot_flops // 2,
        moved=slot_bytes // 2,
    )(index, *blocks, near)
    agg = call(
        functools.partial(aggregate, reps, groups, lists, cap, 1),
        like((reps, part, nodes), BF16),
        [SMEM] + [VMEM] * (reps + 2),
        [pltpu.VMEM((reps, part, nodes), F32)],
        flops=slot_flops // 2,
        moved=slot_bytes // 2,
    )(index, *blocks, far, agg)

    out_rows, dagg, terms = call(
        functools.partial(dense_layer, reps),
        [
            like((nodes, width), BF16),
            like((reps, nodes, width), BF16),
            like((2, width // 2, width), BF16),
        ],
        [VMEM] * (reps + 3),
        [
            pltpu.VMEM((reps, reps, part, nodes), BF16),
            pltpu.VMEM((reps, nodes, width), BF16),
            pltpu.VMEM((reps, nodes, width), BF16),
        ],
        flops=6 * reps * nodes * width * width,
        moved=2 * reps * 5 * nodes * width,
    )(*direct([agg] * reps), cotangents, swap(cotangents, "rep", 1), weight)

    send = call(
        functools.partial(feature_grads, reps, groups, lists, cap, 1),
        like((half + width // 2 // nodes, nodes, width), BF16),
        [SMEM] + [VMEM] * (reps + 2),
        [pltpu.VMEM((half, nodes, width), F32)],
        flops=slot_flops // 2,
        moved=slot_bytes // 2,
    )(index, *blocks, dagg, terms)
    keep = call(
        functools.partial(feature_grads, reps, groups, lists, cap, 0),
        like((half, nodes, width), F32),
        [SMEM] + [VMEM] * (reps + 1),
        flops=slot_flops // 2,
        moved=slot_bytes // 2,
    )(index, *blocks, dagg)
    own, own_terms, *sends = call(
        functools.partial(add_core, half),
        [like((nodes, width), F32), like((width // 2, width), BF16)]
        + [like((nodes + width // 2, width), BF16)] * (half - 1),
        [VMEM] * 3,
        moved=10 * half * nodes * width,
    )(keep, terms, swap(send, "blk", 1))
    grads, terms = call(
        functools.partial(add_chips, half),
        [like((nodes, width), F32), like((width // 2, width), F32)],
        [VMEM] * (half + 1),
        [pltpu.VMEM((half, width // 2, width), F32)],
        moved=8 * half * nodes * width,
    )(own, own_terms, *[swap(sends[half - 1 - k], "blk", 2 * k) for k in range(half - 1, 0, -1)])
    grad_feats, out_rows = call(
        store,
        [like((nodes, width), F32), like((nodes, width), BF16)],
        [VMEM] * 2,
        moved=12 * nodes * width,
    )(grads, out_rows)
    grad_weight = call(
        join_cores, like((width, width), F32), [VMEM] * 2, moved=8 * width * width
    )(terms, swap(terms, "blk", 1))
    return (out_rows, grad_weight, grad_feats)


def solution(mesh):
    return jax.shard_map(
        per_device,
        mesh=mesh,
        in_specs=(
            P(("blk", "rep"), None),
            P(),
            P(("blk", "rep"), None),
            P("blk", "rep", None, None, None, None),
            P("blk", "rep", None, None),
            P("blk", "rep", None, None),
            P("blk", "rep", None),
        ),
        out_specs=(P(("blk", "rep"), None), P(), P(("blk", "rep"), None)),
        check_vma=False,
    )
```

```python
import functools

import jax
import jax.numpy as jnp
from jax import lax
from jax.experimental import pallas as pl
from jax.experimental.pallas import tpu as pltpu
from jax.sharding import PartitionSpec as P

F32 = jnp.float32
BF16 = jnp.bfloat16
VMEM = pl.BlockSpec(memory_space=pltpu.VMEM)
SMEM = pl.BlockSpec(memory_space=pltpu.SMEM)
PAD = 16


def swap(array, axis, bit):
    peers = lax.axis_size(axis)
    return lax.ppermute(array, axis, [(i, i ^ bit) for i in range(peers)])


def spread(array, last=1):
    reps = lax.axis_size("rep")
    held = {0: array}
    bit = reps // 2
    while bit >= last:
        held.update({x | bit: swap(part, "rep", bit) for x, part in held.items()})
        bit //= 2
    return [held[x] for x in sorted(held)]


def call(body, outs, in_specs, scratch=(), flops=0, moved=0):
    return pl.pallas_call(
        body,
        out_shape=outs,
        in_specs=in_specs,
        out_specs=jax.tree.map(lambda _: VMEM, outs),
        scratch_shapes=list(scratch),
        compiler_params=pltpu.CompilerParams(vmem_limit_bytes=48 * 1024 * 1024),
        cost_estimate=pl.CostEstimate(flops=flops, bytes_accessed=moved, transcendentals=0),
    )


def dot(a, b, a_dim, b_dim):
    return lax.dot_general(a, b, (((a_dim,), (b_dim,)), ((), ())), preferred_element_type=F32)


def other(axis, by):
    return lax.bitwise_xor(lax.axis_index(axis), by)


def split_features(reps, lists, cap, feats, rows, cols, counts, *rest):
    outs, turned = rest[:-1], rest[-1]
    nodes = feats.shape[0]
    part = feats.shape[1] // reps
    turned[...] = feats[...].astype(F32).T.astype(BF16).reshape(turned.shape)
    lane = lax.broadcasted_iota(jnp.int32, (PAD, nodes), 1)
    index = jnp.zeros((PAD, nodes), jnp.int32)
    slots = lists * cap
    for j in range(lists):
        for c in range(cap):
            k = j * cap + c
            index = jnp.where(lane == k, rows[j, c], index)
            index = jnp.where(lane == slots + k, cols[j, c], index)
        index = jnp.where(lane == 2 * slots + j, counts[j], index)
    index = index.astype(F32).astype(BF16)
    for x in range(reps):
        outs[x][:part] = turned[other("rep", x)]
        outs[x][part:] = index


def order_chunks(reps, part, *refs):
    copies = reps // 2 - 1
    chunks, sources, unread = refs[:reps], refs[reps : reps + copies], refs[reps + copies]
    mine, index = refs[reps + copies + 1 : reps + copies + 3]
    for source, target in zip(sources, refs[reps + copies + 3 :]):
        target[...] = source[...]
    for x in range(reps):
        mine[other("rep", x)] = chunks[x][:part]
        index[x] = chunks[x][part:].astype(F32).astype(jnp.int32)[:1]


def join(half, *refs):
    out, pairs = refs[-2:]
    for k, ref in enumerate(refs[:half]):
        out[k] = ref[...]
    for k in range(pairs.shape[0]):
        pairs[k] = refs[half + k][...]


def slot_of(index, lists, cap, t, j, c):
    k = j * cap + c
    slots = lists * cap
    return index[t, 0, k], index[t, 0, slots + k], c < index[t, 0, 2 * slots + j]


def relative(groups, lists, x, j):
    mine = lax.axis_index("blk")
    offset = other("rep", x) * lists + j
    return lax.div(lax.bitwise_xor(mine, lax.rem(mine + groups - offset, groups)), 2)


def aggregate(reps, groups, lists, cap, parity, index, *refs):
    blocks, held, start, out = refs[:reps], refs[reps], refs[reps + 1 : -2], refs[-2]
    total = refs[-1]
    total[...] = start[0][...] if start else jnp.zeros_like(total)
    for x in range(reps):
        for j in range(parity, lists, 2):
            place = relative(groups, lists, x, j)
            for c in range(cap):
                row, col, live = slot_of(index, lists, cap, x, j, c)
                product = dot(held[place, col], blocks[x][j * cap + c], 1, 1)
                total[row] += jnp.where(live, product, 0.0)
    out[...] = total[...].astype(out.dtype)


def dense_layer(reps, *refs):
    chunks = refs[:reps]
    cotangents = refs[reps : reps + 2]
    weight, out, dagg, terms, agg, cot, outs = refs[reps + 2 :]
    nodes, width = out.shape
    for x in range(reps):
        origin = other("rep", x)
        cot[origin] = cotangents[x % 2][x // 2]
        for b in range(reps):
            agg[b, origin] = chunks[x][b]
    gw = jnp.zeros((width, width), F32)
    for b in range(reps):
        turned = agg[b].reshape(width, nodes)
        pre = dot(turned, weight[...], 0, 0)
        sigma = jax.nn.sigmoid(pre)
        outs[b] = (pre * sigma).astype(BF16)
        slope = sigma * (1.0 + pre * (1.0 - sigma))
        dpre = (cot[b].astype(F32) * slope).astype(BF16)
        dagg[b] = dot(dpre, weight[...], 1, 1).astype(BF16)
        gw += dot(turned, dpre, 1, 0)
    out[...] = outs[lax.axis_index("rep")]
    terms[...] = gw.astype(BF16).reshape(terms.shape)


def feature_grads(reps, groups, lists, cap, parity, index, *refs):
    blocks, dagg, rest = refs[:reps], refs[reps], refs[reps + 1 :]
    me = lax.axis_index("rep")
    half = groups // 2
    total = rest[-1]
    total[...] = jnp.zeros_like(total)
    for x in range(reps):
        for j in range(parity, lists, 2):
            place = relative(groups, lists, x, j)
            for c in range(cap):
                row, col, live = slot_of(index, lists, cap, x, j, c)

                @pl.when(jnp.logical_and(live, col == me))
                def _():
                    total[place] += dot(blocks[x][j * cap + c], dagg[row], 0, 0)

    if parity:
        terms, send = rest[:2]
        send[:half] = total[...].astype(BF16)
        core = lax.rem(lax.axis_index("blk"), 2)
        send[half:] = terms[1 - core].reshape(-1, *send.shape[1:])


def dense_and_send(reps, groups, lists, cap, index, *refs):
    blocks, rest = refs[:reps], refs[reps:]
    sources, weight, out, dagg, terms, send = rest[:-9], *rest[-9:-4]
    agg, cot, outs, total = rest[-4:]
    dense_layer(reps, *sources, weight, out, dagg, terms, agg, cot, outs)
    feature_grads(reps, groups, lists, cap, 1, index, *blocks, dagg, terms, send, total)


def add_core(half, keep, terms, arrived, own, own_terms, *sends):
    nodes = own.shape[0]
    own[...] = keep[0] + arrived[0].astype(F32)
    core = lax.rem(lax.axis_index("blk"), 2)
    mine = terms[core].astype(F32)
    gw = (mine + arrived[half:].reshape(mine.shape).astype(F32)).astype(BF16)
    own_terms[...] = gw
    for k in range(1, half):
        sends[half - 1 - k][:nodes] = (keep[k] + arrived[k].astype(F32)).astype(BF16)
        sends[half - 1 - k][nodes:] = gw


def add_chips(half, own, own_terms, *refs):
    parts, grads, terms, held = refs[: half - 1], refs[-3], refs[-2], refs[-1]
    nodes = own.shape[0]
    chip = lax.div(lax.axis_index("blk"), 2)
    total = own[...]
    held[chip] = own_terms[...].astype(F32)
    for k in range(1, half):
        total += parts[half - 1 - k][:nodes].astype(F32)
        held[lax.bitwise_xor(chip, k)] = parts[half - 1 - k][nodes:].astype(F32)
    grads[...] = total
    gw = held[0]
    for k in range(1, half):
        gw += held[k]
    terms[...] = gw


def store(grads, rows, grad_feats, out_rows):
    grad_feats[...] = grads[...]
    out_rows[...] = rows[...]


def join_cores(mine, arrived, out):
    core = lax.rem(lax.axis_index("blk"), 2)
    rows = mine.shape[0]
    out[pl.ds(pl.multiple_of(core * rows, rows), rows), :] = mine[...]
    out[pl.ds(pl.multiple_of((1 - core) * rows, rows), rows), :] = arrived[...]


def per_device(feats, weight, cotangent, block_vals, block_rows, block_cols, step_counts):
    reps = lax.axis_size("rep")
    groups = lax.axis_size("blk")
    lists, cap, block = block_vals.shape[2:5]
    nodes, width = feats.shape
    part = width // reps
    slots = lists * cap
    half = groups // 2
    like = jax.ShapeDtypeStruct

    def direct(arrays):
        return [arrays[0]] + [swap(arrays[x], "rep", x) for x in range(1, reps)]

    adjacency = block_vals.reshape(slots, block, block)
    evens = spread(adjacency, 2)
    odds = [swap(adjacency, "rep", 1)]
    chunks = call(
        functools.partial(split_features, reps, lists, cap),
        [like((part + PAD, nodes), BF16)] * reps,
        [VMEM, SMEM, SMEM, SMEM],
        [pltpu.VMEM((reps, part, nodes), BF16)],
        moved=4 * nodes * width,
    )(feats, block_rows[0, 0], block_cols[0, 0], step_counts[0, 0])
    mine, index, *relayed = call(
        functools.partial(order_chunks, reps, part),
        [like((reps, part, nodes), BF16), like((reps, 1, nodes), jnp.int32)]
        + [like((slots, block, block), BF16)] * (reps // 2 - 1),
        [VMEM] * (reps + reps // 2 - 1) + [pl.BlockSpec(memory_space=pl.ANY)],
        moved=4 * nodes * width,
    )(*direct(chunks), *evens[1:], odds[0])
    odds += [swap(array, "rep", 1) for array in relayed]
    blocks = [array for pair in zip(evens, odds) for array in pair]

    near, cotangents = call(
        functools.partial(join, half),
        [like((half, reps, part, nodes), BF16), like((reps // 2, nodes, width), BF16)],
        [VMEM] * (half + reps // 2) + [pl.BlockSpec(memory_space=pl.ANY)] * (reps // 2 - 1),
        moved=4 * half * nodes * width,
    )(
        mine,
        *[swap(mine, "blk", 2 * k) for k in range(1, half)],
        *spread(cotangent, 2),
        *odds[1:],
    )
    far = swap(near, "blk", 1)
    slot_flops = 2 * groups * cap * part * block * block
    slot_bytes = 2 * (groups * cap * block * block + groups * nodes * width)

    agg = call(
        functools.partial(aggregate, reps, groups, lists, cap, 0),
        like((reps, part, nodes), F32),
        [SMEM] + [VMEM] * (reps + 1),
        [pltpu.VMEM((reps, part, nodes), F32)],
        flops=slot_flops // 2,
        moved=slot_bytes // 2,
    )(index, *blocks, near)
    agg = call(
        functools.partial(aggregate, reps, groups, lists, cap, 1),
        like((reps, part, nodes), BF16),
        [SMEM] + [VMEM] * (reps + 2),
        [pltpu.VMEM((reps, part, nodes), F32)],
        flops=slot_flops // 2,
        moved=slot_bytes // 2,
    )(index, *blocks, far, agg)

    out_rows, dagg, terms, send = call(
        functools.partial(dense_and_send, reps, groups, lists, cap),
        [
            like((nodes, width), BF16),
            like((reps, nodes, width), BF16),
            like((2, width // 2, width), BF16),
            like((half + width // 2 // nodes, nodes, width), BF16),
        ],
        [SMEM] + [VMEM] * (2 * reps + 3),
        [
            pltpu.VMEM((reps, reps, part, nodes), BF16),
            pltpu.VMEM((reps, nodes, width), BF16),
            pltpu.VMEM((reps, nodes, width), BF16),
            pltpu.VMEM((half, nodes, width), F32),
        ],
        flops=6 * reps * nodes * width * width + slot_flops // 2,
        moved=2 * reps * 5 * nodes * width + slot_bytes // 2,
    )(index, *blocks, *direct([agg] * reps), cotangents, swap(cotangents, "rep", 1), weight)

    keep = call(
        functools.partial(feature_grads, reps, groups, lists, cap, 0),
        like((half, nodes, width), F32),
        [SMEM] + [VMEM] * (reps + 1),
        flops=slot_flops // 2,
        moved=slot_bytes // 2,
    )(index, *blocks, dagg)
    own, own_terms, *sends = call(
        functools.partial(add_core, half),
        [like((nodes, width), F32), like((width // 2, width), BF16)]
        + [like((nodes + width // 2, width), BF16)] * (half - 1),
        [VMEM] * 3,
        moved=10 * half * nodes * width,
    )(keep, terms, swap(send, "blk", 1))
    grads, terms = call(
        functools.partial(add_chips, half),
        [like((nodes, width), F32), like((width // 2, width), F32)],
        [VMEM] * (half + 1),
        [pltpu.VMEM((half, width // 2, width), F32)],
        moved=8 * half * nodes * width,
    )(own, own_terms, *[swap(sends[half - 1 - k], "blk", 2 * k) for k in range(half - 1, 0, -1)])
    grad_feats, out_rows = call(
        store,
        [like((nodes, width), F32), like((nodes, width), BF16)],
        [VMEM] * 2,
        moved=12 * nodes * width,
    )(grads, out_rows)
    grad_weight = call(
        join_cores, like((width, width), F32), [VMEM] * 2, moved=8 * width * width
    )(terms, swap(terms, "blk", 1))
    return (out_rows, grad_weight, grad_feats)


def solution(mesh):
    return jax.shard_map(
        per_device,
        mesh=mesh,
        in_specs=(
            P(("blk", "rep"), None),
            P(),
            P(("blk", "rep"), None),
            P("blk", "rep", None, None, None, None),
            P("blk", "rep", None, None),
            P("blk", "rep", None, None),
            P("blk", "rep", None),
        ),
        out_specs=(P(("blk", "rep"), None), P(), P(("blk", "rep"), None)),
        check_vma=False,
    )
```

```python
import functools

import jax
import jax.numpy as jnp
from jax import lax
from jax.experimental import pallas as pl
from jax.experimental.pallas import tpu as pltpu
from jax.sharding import PartitionSpec as P

F32 = jnp.float32
BF16 = jnp.bfloat16
VMEM = pl.BlockSpec(memory_space=pltpu.VMEM)
SMEM = pl.BlockSpec(memory_space=pltpu.SMEM)
PAD = 16


def swap(array, axis, bit):
    peers = lax.axis_size(axis)
    return lax.ppermute(array, axis, [(i, i ^ bit) for i in range(peers)])


def spread(array, last=1):
    reps = lax.axis_size("rep")
    held = {0: array}
    bit = reps // 2
    while bit >= last:
        held.update({x | bit: swap(part, "rep", bit) for x, part in held.items()})
        bit //= 2
    return [held[x] for x in sorted(held)]


def call(body, outs, in_specs, scratch=(), flops=0, moved=0):
    return pl.pallas_call(
        body,
        out_shape=outs,
        in_specs=in_specs,
        out_specs=jax.tree.map(lambda _: VMEM, outs),
        scratch_shapes=list(scratch),
        compiler_params=pltpu.CompilerParams(vmem_limit_bytes=48 * 1024 * 1024),
        cost_estimate=pl.CostEstimate(flops=flops, bytes_accessed=moved, transcendentals=0),
    )


def dot(a, b, a_dim, b_dim):
    return lax.dot_general(a, b, (((a_dim,), (b_dim,)), ((), ())), preferred_element_type=F32)


def other(axis, by):
    return lax.bitwise_xor(lax.axis_index(axis), by)


def split_features(reps, lists, cap, feats, rows, cols, counts, *rest):
    outs, turned = rest[:-1], rest[-1]
    nodes = feats.shape[0]
    part = feats.shape[1] // reps
    turned[...] = feats[...].astype(F32).T.astype(BF16).reshape(turned.shape)
    lane = lax.broadcasted_iota(jnp.int32, (PAD, nodes), 1)
    index = jnp.zeros((PAD, nodes), jnp.int32)
    slots = lists * cap
    for j in range(lists):
        for c in range(cap):
            k = j * cap + c
            index = jnp.where(lane == k, rows[j, c], index)
            index = jnp.where(lane == slots + k, cols[j, c], index)
        index = jnp.where(lane == 2 * slots + j, counts[j], index)
    index = index.astype(F32).astype(BF16)
    for x in range(reps):
        outs[x][:part] = turned[other("rep", x)]
        outs[x][part:] = index


def order_chunks(reps, part, *refs):
    copies = reps // 2 - 1
    chunks, unread, sources = refs[:reps], refs[reps], refs[reps + 1 : reps + 1 + copies]
    mine, index = refs[reps + copies + 1 : reps + copies + 3]
    for source, target in zip(sources, refs[reps + copies + 3 :]):
        target[...] = source[...]
    for x in range(reps):
        mine[other("rep", x)] = chunks[x][:part]
        index[x] = chunks[x][part:].astype(F32).astype(jnp.int32)[:1]


def join(half, *refs):
    out, pairs = refs[-2:]
    for k, ref in enumerate(refs[:half]):
        out[k] = ref[...]
    for k in range(pairs.shape[0]):
        pairs[k] = refs[half + k][...]


def slot_of(index, lists, cap, t, j, c):
    k = j * cap + c
    slots = lists * cap
    return index[t, 0, k], index[t, 0, slots + k], c < index[t, 0, 2 * slots + j]


def relative(groups, lists, x, j):
    mine = lax.axis_index("blk")
    offset = other("rep", x) * lists + j
    return lax.div(lax.bitwise_xor(mine, lax.rem(mine + groups - offset, groups)), 2)


def aggregate(reps, groups, lists, cap, parity, index, *refs):
    blocks, held, start, out = refs[:reps], refs[reps], refs[reps + 1 : -2], refs[-2]
    total = refs[-1]
    total[...] = start[0][...] if start else jnp.zeros_like(total)
    for x in range(reps):
        for j in range(parity, lists, 2):
            place = relative(groups, lists, x, j)
            for c in range(cap):
                row, col, live = slot_of(index, lists, cap, x, j, c)
                product = dot(held[place, col], blocks[x][j * cap + c], 1, 1)
                total[row] += jnp.where(live, product, 0.0)
    out[...] = total[...].astype(out.dtype)


def dense_layer(reps, *refs):
    chunks = refs[:reps]
    cotangents = refs[reps : reps + 2]
    weight, out, dagg, terms, agg, cot, outs = refs[reps + 2 :]
    nodes, width = out.shape
    for x in range(reps):
        origin = other("rep", x)
        cot[origin] = cotangents[x % 2][x // 2]
        for b in range(reps):
            agg[b, origin] = chunks[x][b]
    gw = jnp.zeros((width, width), F32)
    for b in range(reps):
        turned = agg[b].reshape(width, nodes)
        pre = dot(turned, weight[...], 0, 0)
        sigma = jax.nn.sigmoid(pre)
        outs[b] = (pre * sigma).astype(BF16)
        slope = sigma * (1.0 + pre * (1.0 - sigma))
        dpre = (cot[b].astype(F32) * slope).astype(BF16)
        dagg[b] = dot(dpre, weight[...], 1, 1).astype(BF16)
        gw += dot(turned, dpre, 1, 0)
    out[...] = outs[lax.axis_index("rep")]
    terms[...] = gw.astype(BF16).reshape(terms.shape)


def feature_grads(reps, groups, lists, cap, parity, index, *refs):
    blocks, dagg, rest = refs[:reps], refs[reps], refs[reps + 1 :]
    me = lax.axis_index("rep")
    half = groups // 2
    total = rest[-1]
    total[...] = jnp.zeros_like(total)
    for x in range(reps):
        for j in range(parity, lists, 2):
            place = relative(groups, lists, x, j)
            for c in range(cap):
                row, col, live = slot_of(index, lists, cap, x, j, c)

                @pl.when(jnp.logical_and(live, col == me))
                def _():
                    total[place] += dot(blocks[x][j * cap + c], dagg[row], 0, 0)

    if parity:
        terms, send = rest[:2]
        send[:half] = total[...].astype(BF16)
        core = lax.rem(lax.axis_index("blk"), 2)
        send[half:] = terms[1 - core].reshape(-1, *send.shape[1:])


def add_core(half, keep, terms, arrived, own, own_terms, *sends):
    nodes = own.shape[0]
    own[...] = keep[0] + arrived[0].astype(F32)
    core = lax.rem(lax.axis_index("blk"), 2)
    mine = terms[core].astype(F32)
    gw = (mine + arrived[half:].reshape(mine.shape).astype(F32)).astype(BF16)
    own_terms[...] = gw
    for k in range(1, half):
        sends[half - 1 - k][:nodes] = (keep[k] + arrived[k].astype(F32)).astype(BF16)
        sends[half - 1 - k][nodes:] = gw


def add_chips(half, own, own_terms, *refs):
    parts, grads, terms, held = refs[: half - 1], refs[-3], refs[-2], refs[-1]
    nodes = own.shape[0]
    chip = lax.div(lax.axis_index("blk"), 2)
    total = own[...]
    held[chip] = own_terms[...].astype(F32)
    for k in range(1, half):
        total += parts[half - 1 - k][:nodes].astype(F32)
        held[lax.bitwise_xor(chip, k)] = parts[half - 1 - k][nodes:].astype(F32)
    grads[...] = total
    gw = held[0]
    for k in range(1, half):
        gw += held[k]
    terms[...] = gw


def store(grads, rows, grad_feats, out_rows):
    grad_feats[...] = grads[...]
    out_rows[...] = rows[...]


def join_cores(mine, arrived, out):
    core = lax.rem(lax.axis_index("blk"), 2)
    rows = mine.shape[0]
    out[pl.ds(pl.multiple_of(core * rows, rows), rows), :] = mine[...]
    out[pl.ds(pl.multiple_of((1 - core) * rows, rows), rows), :] = arrived[...]


def per_device(feats, weight, cotangent, block_vals, block_rows, block_cols, step_counts):
    reps = lax.axis_size("rep")
    groups = lax.axis_size("blk")
    lists, cap, block = block_vals.shape[2:5]
    nodes, width = feats.shape
    part = width // reps
    slots = lists * cap
    half = groups // 2
    like = jax.ShapeDtypeStruct

    def direct(arrays):
        return [arrays[0]] + [swap(arrays[x], "rep", x) for x in range(1, reps)]

    adjacency = block_vals.reshape(slots, block, block)
    odds = [swap(adjacency, "rep", 1)]
    evens = spread(adjacency, 2)
    chunks = call(
        functools.partial(split_features, reps, lists, cap),
        [like((part + PAD, nodes), BF16)] * reps,
        [VMEM, SMEM, SMEM, SMEM],
        [pltpu.VMEM((reps, part, nodes), BF16)],
        moved=4 * nodes * width,
    )(feats, block_rows[0, 0], block_cols[0, 0], step_counts[0, 0])
    mine, index, *relayed = call(
        functools.partial(order_chunks, reps, part),
        [like((reps, part, nodes), BF16), like((reps, 1, nodes), jnp.int32)]
        + [like((slots, block, block), BF16)] * (reps // 2 - 1),
        [VMEM] * reps + [pl.BlockSpec(memory_space=pl.ANY)] + [VMEM] * (reps // 2 - 1),
        moved=4 * nodes * width,
    )(*direct(chunks), odds[0], *evens[1:])
    odds += [swap(array, "rep", 1) for array in relayed]
    blocks = [array for pair in zip(evens, odds) for array in pair]

    near, cotangents = call(
        functools.partial(join, half),
        [like((half, reps, part, nodes), BF16), like((reps // 2, nodes, width), BF16)],
        [VMEM] * (half + reps // 2) + [pl.BlockSpec(memory_space=pl.ANY)] * (reps // 2 - 1),
        moved=4 * half * nodes * width,
    )(
        mine,
        *[swap(mine, "blk", 2 * k) for k in range(1, half)],
        *spread(cotangent, 2),
        *odds[1:],
    )
    far = swap(near, "blk", 1)
    slot_flops = 2 * groups * cap * part * block * block
    slot_bytes = 2 * (groups * cap * block * block + groups * nodes * width)

    agg = call(
        functools.partial(aggregate, reps, groups, lists, cap, 0),
        like((reps, part, nodes), F32),
        [SMEM] + [VMEM] * (reps + 1),
        [pltpu.VMEM((reps, part, nodes), F32)],
        flops=slot_flops // 2,
        moved=slot_bytes // 2,
    )(index, *blocks, near)
    agg = call(
        functools.partial(aggregate, reps, groups, lists, cap, 1),
        like((reps, part, nodes), BF16),
        [SMEM] + [VMEM] * (reps + 2),
        [pltpu.VMEM((reps, part, nodes), F32)],
        flops=slot_flops // 2,
        moved=slot_bytes // 2,
    )(index, *blocks, far, agg)

    out_rows, dagg, terms = call(
        functools.partial(dense_layer, reps),
        [
            like((nodes, width), BF16),
            like((reps, nodes, width), BF16),
            like((2, width // 2, width), BF16),
        ],
        [VMEM] * (reps + 3),
        [
            pltpu.VMEM((reps, reps, part, nodes), BF16),
            pltpu.VMEM((reps, nodes, width), BF16),
            pltpu.VMEM((reps, nodes, width), BF16),
        ],
        flops=6 * reps * nodes * width * width,
        moved=2 * reps * 5 * nodes * width,
    )(*direct([agg] * reps), cotangents, swap(cotangents, "rep", 1), weight)

    send = call(
        functools.partial(feature_grads, reps, groups, lists, cap, 1),
        like((half + width // 2 // nodes, nodes, width), BF16),
        [SMEM] + [VMEM] * (reps + 2),
        [pltpu.VMEM((half, nodes, width), F32)],
        flops=slot_flops // 2,
        moved=slot_bytes // 2,
    )(index, *blocks, dagg, terms)
    keep = call(
        functools.partial(feature_grads, reps, groups, lists, cap, 0),
        like((half, nodes, width), F32),
        [SMEM] + [VMEM] * (reps + 1),
        flops=slot_flops // 2,
        moved=slot_bytes // 2,
    )(index, *blocks, dagg)
    own, own_terms, *sends = call(
        functools.partial(add_core, half),
        [like((nodes, width), F32), like((width // 2, width), BF16)]
        + [like((nodes + width // 2, width), BF16)] * (half - 1),
        [VMEM] * 3,
        moved=10 * half * nodes * width,
    )(keep, terms, swap(send, "blk", 1))
    grads, terms = call(
        functools.partial(add_chips, half),
        [like((nodes, width), F32), like((width // 2, width), F32)],
        [VMEM] * (half + 1),
        [pltpu.VMEM((half, width // 2, width), F32)],
        moved=8 * half * nodes * width,
    )(own, own_terms, *[swap(sends[half - 1 - k], "blk", 2 * k) for k in range(half - 1, 0, -1)])
    grad_feats, out_rows = call(
        store,
        [like((nodes, width), F32), like((nodes, width), BF16)],
        [VMEM] * 2,
        moved=12 * nodes * width,
    )(grads, out_rows)
    grad_weight = call(
        join_cores, like((width, width), F32), [VMEM] * 2, moved=8 * width * width
    )(terms, swap(terms, "blk", 1))
    return (out_rows, grad_weight, grad_feats)


def solution(mesh):
    return jax.shard_map(
        per_device,
        mesh=mesh,
        in_specs=(
            P(("blk", "rep"), None),
            P(),
            P(("blk", "rep"), None),
            P("blk", "rep", None, None, None, None),
            P("blk", "rep", None, None),
            P("blk", "rep", None, None),
            P("blk", "rep", None),
        ),
        out_specs=(P(("blk", "rep"), None), P(), P(("blk", "rep"), None)),
        check_vma=False,
    )
```

```python
import functools

import jax
import jax.numpy as jnp
from jax import lax
from jax.experimental import pallas as pl
from jax.experimental.pallas import tpu as pltpu
from jax.sharding import PartitionSpec as P

F32 = jnp.float32
BF16 = jnp.bfloat16
VMEM = pl.BlockSpec(memory_space=pltpu.VMEM)
SMEM = pl.BlockSpec(memory_space=pltpu.SMEM)
PAD = 16


def swap(array, axis, bit):
    peers = lax.axis_size(axis)
    return lax.ppermute(array, axis, [(i, i ^ bit) for i in range(peers)])


def spread(array, last=1):
    reps = lax.axis_size("rep")
    held = {0: array}
    bit = reps // 2
    while bit >= last:
        held.update({x | bit: swap(part, "rep", bit) for x, part in held.items()})
        bit //= 2
    return [held[x] for x in sorted(held)]


def call(body, outs, in_specs, scratch=(), flops=0, moved=0):
    return pl.pallas_call(
        body,
        out_shape=outs,
        in_specs=in_specs,
        out_specs=jax.tree.map(lambda _: VMEM, outs),
        scratch_shapes=list(scratch),
        compiler_params=pltpu.CompilerParams(vmem_limit_bytes=48 * 1024 * 1024),
        cost_estimate=pl.CostEstimate(flops=flops, bytes_accessed=moved, transcendentals=0),
    )


def dot(a, b, a_dim, b_dim):
    return lax.dot_general(a, b, (((a_dim,), (b_dim,)), ((), ())), preferred_element_type=F32)


def other(axis, by):
    return lax.bitwise_xor(lax.axis_index(axis), by)


def split_features(reps, lists, cap, feats, rows, cols, counts, *rest):
    outs, turned = rest[:-1], rest[-1]
    nodes = feats.shape[0]
    part = feats.shape[1] // reps
    turned[...] = feats[...].astype(F32).T.astype(BF16).reshape(turned.shape)
    lane = lax.broadcasted_iota(jnp.int32, (PAD, nodes), 1)
    index = jnp.zeros((PAD, nodes), jnp.int32)
    slots = lists * cap
    for j in range(lists):
        for c in range(cap):
            k = j * cap + c
            index = jnp.where(lane == k, rows[j, c], index)
            index = jnp.where(lane == slots + k, cols[j, c], index)
        index = jnp.where(lane == 2 * slots + j, counts[j], index)
    index = index.astype(F32).astype(BF16)
    for x in range(reps):
        outs[x][:part] = turned[other("rep", x)]
        outs[x][part:] = index


def order_chunks(reps, part, *refs):
    copies = reps // 2 - 1
    chunks, unread, sources = refs[:reps], refs[reps], refs[reps + 1 : reps + 1 + copies]
    mine, index = refs[reps + copies + 1 : reps + copies + 3]
    for source, target in zip(sources, refs[reps + copies + 3 :]):
        target[...] = source[...]
    for x in range(reps):
        mine[other("rep", x)] = chunks[-x][:part]
        index[x] = chunks[-x][part:].astype(F32).astype(jnp.int32)[:1]


def join(half, *refs):
    out, pairs = refs[-2:]
    for k, ref in enumerate(refs[:half]):
        out[k] = ref[...]
    for k in range(pairs.shape[0]):
        pairs[k] = refs[half + k][...]


def slot_of(index, lists, cap, t, j, c):
    k = j * cap + c
    slots = lists * cap
    return index[t, 0, k], index[t, 0, slots + k], c < index[t, 0, 2 * slots + j]


def relative(groups, lists, x, j):
    mine = lax.axis_index("blk")
    offset = other("rep", x) * lists + j
    return lax.div(lax.bitwise_xor(mine, lax.rem(mine + groups - offset, groups)), 2)


def aggregate(reps, groups, lists, cap, parity, index, *refs):
    blocks, held, start, out = refs[:reps], refs[reps], refs[reps + 1 : -2], refs[-2]
    total = refs[-1]
    total[...] = start[0][...] if start else jnp.zeros_like(total)
    for x in range(reps):
        for j in range(parity, lists, 2):
            place = relative(groups, lists, x, j)
            for c in range(cap):
                row, col, live = slot_of(index, lists, cap, x, j, c)
                product = dot(held[place, col], blocks[x][j * cap + c], 1, 1)
                total[row] += jnp.where(live, product, 0.0)
    out[...] = total[...].astype(out.dtype)


def dense_layer(reps, *refs):
    chunks = refs[:reps]
    cotangents = refs[reps : reps + 2]
    weight, out, dagg, terms, agg, cot, outs = refs[reps + 2 :]
    nodes, width = out.shape
    for x in range(reps):
        origin = other("rep", x)
        cot[origin] = cotangents[x % 2][x // 2]
        for b in range(reps):
            agg[b, origin] = chunks[x][b]
    gw = jnp.zeros((width, width), F32)
    for b in range(reps):
        turned = agg[b].reshape(width, nodes)
        pre = dot(turned, weight[...], 0, 0)
        sigma = jax.nn.sigmoid(pre)
        outs[b] = (pre * sigma).astype(BF16)
        slope = sigma * (1.0 + pre * (1.0 - sigma))
        dpre = (cot[b].astype(F32) * slope).astype(BF16)
        dagg[b] = dot(dpre, weight[...], 1, 1).astype(BF16)
        gw += dot(turned, dpre, 1, 0)
    out[...] = outs[lax.axis_index("rep")]
    terms[...] = gw.astype(BF16).reshape(terms.shape)


def feature_grads(reps, groups, lists, cap, parity, index, *refs):
    blocks, dagg, rest = refs[:reps], refs[reps], refs[reps + 1 :]
    me = lax.axis_index("rep")
    half = groups // 2
    total = rest[-1]
    total[...] = jnp.zeros_like(total)
    for x in range(reps):
        for j in range(parity, lists, 2):
            place = relative(groups, lists, x, j)
            for c in range(cap):
                row, col, live = slot_of(index, lists, cap, x, j, c)

                @pl.when(jnp.logical_and(live, col == me))
                def _():
                    total[place] += dot(blocks[x][j * cap + c], dagg[row], 0, 0)

    if parity:
        terms, send = rest[:2]
        send[:half] = total[...].astype(BF16)
        core = lax.rem(lax.axis_index("blk"), 2)
        send[half:] = terms[1 - core].reshape(-1, *send.shape[1:])


def add_core(half, keep, terms, arrived, own, own_terms, *sends):
    nodes = own.shape[0]
    own[...] = keep[0] + arrived[0].astype(F32)
    core = lax.rem(lax.axis_index("blk"), 2)
    mine = terms[core].astype(F32)
    gw = (mine + arrived[half:].reshape(mine.shape).astype(F32)).astype(BF16)
    own_terms[...] = gw
    for k in range(1, half):
        sends[half - 1 - k][:nodes] = (keep[k] + arrived[k].astype(F32)).astype(BF16)
        sends[half - 1 - k][nodes:] = gw


def add_chips(half, own, own_terms, *refs):
    parts, grads, terms, held = refs[: half - 1], refs[-3], refs[-2], refs[-1]
    nodes = own.shape[0]
    chip = lax.div(lax.axis_index("blk"), 2)
    total = own[...]
    held[chip] = own_terms[...].astype(F32)
    for k in range(1, half):
        total += parts[half - 1 - k][:nodes].astype(F32)
        held[lax.bitwise_xor(chip, k)] = parts[half - 1 - k][nodes:].astype(F32)
    grads[...] = total
    gw = held[0]
    for k in range(1, half):
        gw += held[k]
    terms[...] = gw


def store(grads, rows, grad_feats, out_rows):
    grad_feats[...] = grads[...]
    out_rows[...] = rows[...]


def join_cores(mine, arrived, out):
    core = lax.rem(lax.axis_index("blk"), 2)
    rows = mine.shape[0]
    out[pl.ds(pl.multiple_of(core * rows, rows), rows), :] = mine[...]
    out[pl.ds(pl.multiple_of((1 - core) * rows, rows), rows), :] = arrived[...]


def per_device(feats, weight, cotangent, block_vals, block_rows, block_cols, step_counts):
    reps = lax.axis_size("rep")
    groups = lax.axis_size("blk")
    lists, cap, block = block_vals.shape[2:5]
    nodes, width = feats.shape
    part = width // reps
    slots = lists * cap
    half = groups // 2
    like = jax.ShapeDtypeStruct

    def direct(arrays):
        return [arrays[0]] + [swap(arrays[x], "rep", x) for x in range(1, reps)]

    adjacency = block_vals.reshape(slots, block, block)
    odds = [swap(adjacency, "rep", 1)]
    evens = spread(adjacency, 2)
    chunks = call(
        functools.partial(split_features, reps, lists, cap),
        [like((part + PAD, nodes), BF16)] * reps,
        [VMEM, SMEM, SMEM, SMEM],
        [pltpu.VMEM((reps, part, nodes), BF16)],
        moved=4 * nodes * width,
    )(feats, block_rows[0, 0], block_cols[0, 0], step_counts[0, 0])
    mine, index, *relayed = call(
        functools.partial(order_chunks, reps, part),
        [like((reps, part, nodes), BF16), like((reps, 1, nodes), jnp.int32)]
        + [like((slots, block, block), BF16)] * (reps // 2 - 1),
        [VMEM] * reps + [pl.BlockSpec(memory_space=pl.ANY)] + [VMEM] * (reps // 2 - 1),
        moved=4 * nodes * width,
    )(chunks[0], *direct(chunks)[:0:-1], odds[0], *evens[1:])
    odds += [swap(array, "rep", 1) for array in relayed]
    blocks = [array for pair in zip(evens, odds) for array in pair]

    near, cotangents = call(
        functools.partial(join, half),
        [like((half, reps, part, nodes), BF16), like((reps // 2, nodes, width), BF16)],
        [VMEM] * (half + reps // 2) + [pl.BlockSpec(memory_space=pl.ANY)] * (reps // 2 - 1),
        moved=4 * half * nodes * width,
    )(
        mine,
        *[swap(mine, "blk", 2 * k) for k in range(1, half)],
        *spread(cotangent, 2),
        *odds[1:],
    )
    far = swap(near, "blk", 1)
    slot_flops = 2 * groups * cap * part * block * block
    slot_bytes = 2 * (groups * cap * block * block + groups * nodes * width)

    agg = call(
        functools.partial(aggregate, reps, groups, lists, cap, 0),
        like((reps, part, nodes), F32),
        [SMEM] + [VMEM] * (reps + 1),
        [pltpu.VMEM((reps, part, nodes), F32)],
        flops=slot_flops // 2,
        moved=slot_bytes // 2,
    )(index, *blocks, near)
    agg = call(
        functools.partial(aggregate, reps, groups, lists, cap, 1),
        like((reps, part, nodes), BF16),
        [SMEM] + [VMEM] * (reps + 2),
        [pltpu.VMEM((reps, part, nodes), F32)],
        flops=slot_flops // 2,
        moved=slot_bytes // 2,
    )(index, *blocks, far, agg)

    out_rows, dagg, terms = call(
        functools.partial(dense_layer, reps),
        [
            like((nodes, width), BF16),
            like((reps, nodes, width), BF16),
            like((2, width // 2, width), BF16),
        ],
        [VMEM] * (reps + 3),
        [
            pltpu.VMEM((reps, reps, part, nodes), BF16),
            pltpu.VMEM((reps, nodes, width), BF16),
            pltpu.VMEM((reps, nodes, width), BF16),
        ],
        flops=6 * reps * nodes * width * width,
        moved=2 * reps * 5 * nodes * width,
    )(*direct([agg] * reps), cotangents, swap(cotangents, "rep", 1), weight)

    send = call(
        functools.partial(feature_grads, reps, groups, lists, cap, 1),
        like((half + width // 2 // nodes, nodes, width), BF16),
        [SMEM] + [VMEM] * (reps + 2),
        [pltpu.VMEM((half, nodes, width), F32)],
        flops=slot_flops // 2,
        moved=slot_bytes // 2,
    )(index, *blocks, dagg, terms)
    keep = call(
        functools.partial(feature_grads, reps, groups, lists, cap, 0),
        like((half, nodes, width), F32),
        [SMEM] + [VMEM] * (reps + 1),
        flops=slot_flops // 2,
        moved=slot_bytes // 2,
    )(index, *blocks, dagg)
    own, own_terms, *sends = call(
        functools.partial(add_core, half),
        [like((nodes, width), F32), like((width // 2, width), BF16)]
        + [like((nodes + width // 2, width), BF16)] * (half - 1),
        [VMEM] * 3,
        moved=10 * half * nodes * width,
    )(keep, terms, swap(send, "blk", 1))
    grads, terms = call(
        functools.partial(add_chips, half),
        [like((nodes, width), F32), like((width // 2, width), F32)],
        [VMEM] * (half + 1),
        [pltpu.VMEM((half, width // 2, width), F32)],
        moved=8 * half * nodes * width,
    )(own, own_terms, *[swap(sends[half - 1 - k], "blk", 2 * k) for k in range(half - 1, 0, -1)])
    grad_feats, out_rows = call(
        store,
        [like((nodes, width), F32), like((nodes, width), BF16)],
        [VMEM] * 2,
        moved=12 * nodes * width,
    )(grads, out_rows)
    grad_weight = call(
        join_cores, like((width, width), F32), [VMEM] * 2, moved=8 * width * width
    )(terms, swap(terms, "blk", 1))
    return (out_rows, grad_weight, grad_feats)


def solution(mesh):
    return jax.shard_map(
        per_device,
        mesh=mesh,
        in_specs=(
            P(("blk", "rep"), None),
            P(),
            P(("blk", "rep"), None),
            P("blk", "rep", None, None, None, None),
            P("blk", "rep", None, None),
            P("blk", "rep", None, None),
            P("blk", "rep", None),
        ),
        out_specs=(P(("blk", "rep"), None), P(), P(("blk", "rep"), None)),
        check_vma=False,
    )
```

```python
import functools

import jax
import jax.numpy as jnp
from jax import lax
from jax.experimental import pallas as pl
from jax.experimental.pallas import tpu as pltpu
from jax.sharding import PartitionSpec as P

F32 = jnp.float32
BF16 = jnp.bfloat16
VMEM = pl.BlockSpec(memory_space=pltpu.VMEM)
SMEM = pl.BlockSpec(memory_space=pltpu.SMEM)
PAD = 16


def swap(array, axis, bit):
    peers = lax.axis_size(axis)
    return lax.ppermute(array, axis, [(i, i ^ bit) for i in range(peers)])


def spread(array, last=1):
    reps = lax.axis_size("rep")
    held = {0: array}
    bit = reps // 2
    while bit >= last:
        held.update({x | bit: swap(part, "rep", bit) for x, part in held.items()})
        bit //= 2
    return [held[x] for x in sorted(held)]


def call(body, outs, in_specs, scratch=(), flops=0, moved=0):
    return pl.pallas_call(
        body,
        out_shape=outs,
        in_specs=in_specs,
        out_specs=jax.tree.map(lambda _: VMEM, outs),
        scratch_shapes=list(scratch),
        compiler_params=pltpu.CompilerParams(vmem_limit_bytes=48 * 1024 * 1024),
        cost_estimate=pl.CostEstimate(flops=flops, bytes_accessed=moved, transcendentals=0),
    )


def dot(a, b, a_dim, b_dim):
    return lax.dot_general(a, b, (((a_dim,), (b_dim,)), ((), ())), preferred_element_type=F32)


def other(axis, by):
    return lax.bitwise_xor(lax.axis_index(axis), by)


def split_features(reps, lists, cap, feats, rows, cols, counts, *rest):
    outs, turned = rest[:-1], rest[-1]
    nodes = feats.shape[0]
    part = feats.shape[1] // reps
    turned[...] = feats[...].astype(F32).T.astype(BF16).reshape(turned.shape)
    lane = lax.broadcasted_iota(jnp.int32, (PAD, nodes), 1)
    index = jnp.zeros((PAD, nodes), jnp.int32)
    slots = lists * cap
    for j in range(lists):
        for c in range(cap):
            k = j * cap + c
            index = jnp.where(lane == k, rows[j, c], index)
            index = jnp.where(lane == slots + k, cols[j, c], index)
        index = jnp.where(lane == 2 * slots + j, counts[j], index)
    index = index.astype(F32).astype(BF16)
    for x in range(reps):
        outs[x][:part] = turned[other("rep", x)]
        outs[x][part:] = index


def order_chunks(reps, part, *refs):
    copies = reps // 2 - 1
    chunks, unread, sources = refs[:reps], refs[reps], refs[reps + 1 : reps + 1 + copies]
    mine, index = refs[reps + copies + 1 : reps + copies + 3]
    for source, target in zip(sources, refs[reps + copies + 3 :]):
        target[...] = source[...]
    for x in range(reps):
        mine[other("rep", x)] = chunks[x][:part]
        index[x] = chunks[x][part:].astype(F32).astype(jnp.int32)[:1]


def join(half, *refs):
    out, pairs = refs[-2:]
    for k, ref in enumerate(refs[:half]):
        out[k] = ref[...]
    for k in range(pairs.shape[0]):
        pairs[k] = refs[half + k][...]


def slot_of(index, lists, cap, t, j, c):
    k = j * cap + c
    slots = lists * cap
    return index[t, 0, k], index[t, 0, slots + k], c < index[t, 0, 2 * slots + j]


def relative(groups, lists, x, j):
    mine = lax.axis_index("blk")
    offset = other("rep", x) * lists + j
    return lax.div(lax.bitwise_xor(mine, lax.rem(mine + groups - offset, groups)), 2)


def aggregate(reps, groups, lists, cap, parity, index, *refs):
    blocks, held, start, out = refs[:reps], refs[reps], refs[reps + 1 : -2], refs[-2]
    total = refs[-1]
    total[...] = start[0][...] if start else jnp.zeros_like(total)
    for x in range(reps):
        for j in range(parity, lists, 2):
            place = relative(groups, lists, x, j)
            for c in range(cap):
                row, col, live = slot_of(index, lists, cap, x, j, c)
                product = dot(held[place, col], blocks[x][j * cap + c], 1, 1)
                total[row] += jnp.where(live, product, 0.0)
    out[...] = total[...].astype(out.dtype)


def dense_layer(reps, *refs):
    chunks = refs[:reps]
    cotangents = refs[reps : reps + 2]
    weight, out, dagg, terms, agg, cot, outs = refs[reps + 2 :]
    nodes, width = out.shape
    for x in range(reps):
        origin = other("rep", x)
        cot[origin] = cotangents[x % 2][x // 2]
        for b in range(reps):
            agg[b, origin] = chunks[x][b]
    gw = jnp.zeros((width, width), F32)
    for b in range(reps):
        turned = agg[b].reshape(width, nodes)
        pre = dot(turned, weight[...], 0, 0)
        sigma = jax.nn.sigmoid(pre)
        outs[b] = (pre * sigma).astype(BF16)
        slope = sigma * (1.0 + pre * (1.0 - sigma))
        dpre = (cot[b].astype(F32) * slope).astype(BF16)
        dagg[b] = dot(dpre, weight[...], 1, 1).astype(BF16)
        gw += dot(turned, dpre, 1, 0)
    out[...] = outs[lax.axis_index("rep")]
    terms[...] = gw.astype(BF16).reshape(terms.shape)


def feature_grads(reps, groups, lists, cap, parity, index, *refs):
    blocks, dagg, rest = refs[:reps], refs[reps], refs[reps + 1 :]
    me = lax.axis_index("rep")
    half = groups // 2
    total = rest[-1]
    total[...] = jnp.zeros_like(total)
    for x in range(reps):
        for j in range(parity, lists, 2):
            place = relative(groups, lists, x, j)
            for c in range(cap):
                row, col, live = slot_of(index, lists, cap, x, j, c)

                @pl.when(jnp.logical_and(live, col == me))
                def _():
                    total[place] += dot(blocks[x][j * cap + c], dagg[row], 0, 0)

    if parity:
        terms, send = rest[:2]
        send[:half] = total[...].astype(BF16)
        core = lax.rem(lax.axis_index("blk"), 2)
        send[half:] = terms[1 - core].reshape(-1, *send.shape[1:])


def add_core(half, keep, terms, arrived, own, own_terms, *sends):
    nodes = own.shape[0]
    own[...] = keep[0] + arrived[0].astype(F32)
    core = lax.rem(lax.axis_index("blk"), 2)
    mine = terms[core].astype(F32)
    gw = (mine + arrived[half:].reshape(mine.shape).astype(F32)).astype(BF16)
    own_terms[...] = gw
    for k in range(1, half):
        sends[half - 1 - k][:nodes] = (keep[k] + arrived[k].astype(F32)).astype(BF16)
        sends[half - 1 - k][nodes:] = gw


def add_chips(half, own, own_terms, *refs):
    parts, grads, terms, held = refs[: half - 1], refs[-3], refs[-2], refs[-1]
    nodes = own.shape[0]
    chip = lax.div(lax.axis_index("blk"), 2)
    total = own[...]
    held[chip] = own_terms[...].astype(F32)
    for k in range(1, half):
        total += parts[half - 1 - k][:nodes].astype(F32)
        held[lax.bitwise_xor(chip, k)] = parts[half - 1 - k][nodes:].astype(F32)
    grads[...] = total
    gw = held[0]
    for k in range(1, half):
        gw += held[k]
    terms[...] = gw.astype(BF16)


def store(grads, rows, grad_feats, out_rows):
    grad_feats[...] = grads[...]
    out_rows[...] = rows[...]


def join_cores(mine, arrived, out):
    core = lax.rem(lax.axis_index("blk"), 2)
    rows = mine.shape[0]
    out[pl.ds(pl.multiple_of(core * rows, rows), rows), :] = mine[...].astype(F32)
    out[pl.ds(pl.multiple_of((1 - core) * rows, rows), rows), :] = arrived[...].astype(F32)


def per_device(feats, weight, cotangent, block_vals, block_rows, block_cols, step_counts):
    reps = lax.axis_size("rep")
    groups = lax.axis_size("blk")
    lists, cap, block = block_vals.shape[2:5]
    nodes, width = feats.shape
    part = width // reps
    slots = lists * cap
    half = groups // 2
    like = jax.ShapeDtypeStruct

    def direct(arrays):
        return [arrays[0]] + [swap(arrays[x], "rep", x) for x in range(1, reps)]

    adjacency = block_vals.reshape(slots, block, block)
    odds = [swap(adjacency, "rep", 1)]
    evens = spread(adjacency, 2)
    chunks = call(
        functools.partial(split_features, reps, lists, cap),
        [like((part + PAD, nodes), BF16)] * reps,
        [VMEM, SMEM, SMEM, SMEM],
        [pltpu.VMEM((reps, part, nodes), BF16)],
        moved=4 * nodes * width,
    )(feats, block_rows[0, 0], block_cols[0, 0], step_counts[0, 0])
    mine, index, *relayed = call(
        functools.partial(order_chunks, reps, part),
        [like((reps, part, nodes), BF16), like((reps, 1, nodes), jnp.int32)]
        + [like((slots, block, block), BF16)] * (reps // 2 - 1),
        [VMEM] * reps + [pl.BlockSpec(memory_space=pl.ANY)] + [VMEM] * (reps // 2 - 1),
        moved=4 * nodes * width,
    )(*direct(chunks), odds[0], *evens[1:])
    odds += [swap(array, "rep", 1) for array in relayed]
    blocks = [array for pair in zip(evens, odds) for array in pair]

    near, cotangents = call(
        functools.partial(join, half),
        [like((half, reps, part, nodes), BF16), like((reps // 2, nodes, width), BF16)],
        [VMEM] * (half + reps // 2) + [pl.BlockSpec(memory_space=pl.ANY)] * (reps // 2 - 1),
        moved=4 * half * nodes * width,
    )(
        mine,
        *[swap(mine, "blk", 2 * k) for k in range(1, half)],
        *spread(cotangent, 2),
        *odds[1:],
    )
    far = swap(near, "blk", 1)
    slot_flops = 2 * groups * cap * part * block * block
    slot_bytes = 2 * (groups * cap * block * block + groups * nodes * width)

    agg = call(
        functools.partial(aggregate, reps, groups, lists, cap, 0),
        like((reps, part, nodes), F32),
        [SMEM] + [VMEM] * (reps + 1),
        [pltpu.VMEM((reps, part, nodes), F32)],
        flops=slot_flops // 2,
        moved=slot_bytes // 2,
    )(index, *blocks, near)
    agg = call(
        functools.partial(aggregate, reps, groups, lists, cap, 1),
        like((reps, part, nodes), BF16),
        [SMEM] + [VMEM] * (reps + 2),
        [pltpu.VMEM((reps, part, nodes), F32)],
        flops=slot_flops // 2,
        moved=slot_bytes // 2,
    )(index, *blocks, far, agg)

    out_rows, dagg, terms = call(
        functools.partial(dense_layer, reps),
        [
            like((nodes, width), BF16),
            like((reps, nodes, width), BF16),
            like((2, width // 2, width), BF16),
        ],
        [VMEM] * (reps + 3),
        [
            pltpu.VMEM((reps, reps, part, nodes), BF16),
            pltpu.VMEM((reps, nodes, width), BF16),
            pltpu.VMEM((reps, nodes, width), BF16),
        ],
        flops=6 * reps * nodes * width * width,
        moved=2 * reps * 5 * nodes * width,
    )(*direct([agg] * reps), cotangents, swap(cotangents, "rep", 1), weight)

    send = call(
        functools.partial(feature_grads, reps, groups, lists, cap, 1),
        like((half + width // 2 // nodes, nodes, width), BF16),
        [SMEM] + [VMEM] * (reps + 2),
        [pltpu.VMEM((half, nodes, width), F32)],
        flops=slot_flops // 2,
        moved=slot_bytes // 2,
    )(index, *blocks, dagg, terms)
    keep = call(
        functools.partial(feature_grads, reps, groups, lists, cap, 0),
        like((half, nodes, width), F32),
        [SMEM] + [VMEM] * (reps + 1),
        flops=slot_flops // 2,
        moved=slot_bytes // 2,
    )(index, *blocks, dagg)
    own, own_terms, *sends = call(
        functools.partial(add_core, half),
        [like((nodes, width), F32), like((width // 2, width), BF16)]
        + [like((nodes + width // 2, width), BF16)] * (half - 1),
        [VMEM] * 3,
        moved=10 * half * nodes * width,
    )(keep, terms, swap(send, "blk", 1))
    grads, terms = call(
        functools.partial(add_chips, half),
        [like((nodes, width), F32), like((width // 2, width), BF16)],
        [VMEM] * (half + 1),
        [pltpu.VMEM((half, width // 2, width), F32)],
        moved=8 * half * nodes * width,
    )(own, own_terms, *[swap(sends[half - 1 - k], "blk", 2 * k) for k in range(half - 1, 0, -1)])
    grad_feats, out_rows = call(
        store,
        [like((nodes, width), F32), like((nodes, width), BF16)],
        [VMEM] * 2,
        moved=12 * nodes * width,
    )(grads, out_rows)
    grad_weight = call(
        join_cores, like((width, width), F32), [VMEM] * 2, moved=8 * width * width
    )(terms, swap(terms, "blk", 1))
    return (out_rows, grad_weight, grad_feats)


def solution(mesh):
    return jax.shard_map(
        per_device,
        mesh=mesh,
        in_specs=(
            P(("blk", "rep"), None),
            P(),
            P(("blk", "rep"), None),
            P("blk", "rep", None, None, None, None),
            P("blk", "rep", None, None),
            P("blk", "rep", None, None),
            P("blk", "rep", None),
        ),
        out_specs=(P(("blk", "rep"), None), P(), P(("blk", "rep"), None)),
        check_vma=False,
    )
```

```python
import functools

import jax
import jax.numpy as jnp
from jax import lax
from jax.experimental import pallas as pl
from jax.experimental.pallas import tpu as pltpu
from jax.sharding import PartitionSpec as P

F32 = jnp.float32
BF16 = jnp.bfloat16
VMEM = pl.BlockSpec(memory_space=pltpu.VMEM)
SMEM = pl.BlockSpec(memory_space=pltpu.SMEM)
PAD = 16


def swap(array, axis, bit):
    peers = lax.axis_size(axis)
    return lax.ppermute(array, axis, [(i, i ^ bit) for i in range(peers)])


def spread(array, last=1):
    reps = lax.axis_size("rep")
    held = {0: array}
    bit = reps // 2
    while bit >= last:
        held.update({x | bit: swap(part, "rep", bit) for x, part in held.items()})
        bit //= 2
    return [held[x] for x in sorted(held)]


def call(body, outs, in_specs, scratch=(), flops=0, moved=0):
    return pl.pallas_call(
        body,
        out_shape=outs,
        in_specs=in_specs,
        out_specs=jax.tree.map(lambda _: VMEM, outs),
        scratch_shapes=list(scratch),
        compiler_params=pltpu.CompilerParams(vmem_limit_bytes=48 * 1024 * 1024),
        cost_estimate=pl.CostEstimate(flops=flops, bytes_accessed=moved, transcendentals=0),
    )


def dot(a, b, a_dim, b_dim):
    return lax.dot_general(a, b, (((a_dim,), (b_dim,)), ((), ())), preferred_element_type=F32)


def other(axis, by):
    return lax.bitwise_xor(lax.axis_index(axis), by)


def split_features(reps, lists, cap, feats, rows, cols, counts, *rest):
    outs, turned = rest[:-1], rest[-1]
    nodes = feats.shape[0]
    part = feats.shape[1] // reps
    turned[...] = feats[...].astype(F32).T.astype(BF16).reshape(turned.shape)
    lane = lax.broadcasted_iota(jnp.int32, (PAD, nodes), 1)
    index = jnp.zeros((PAD, nodes), jnp.int32)
    slots = lists * cap
    for j in range(lists):
        for c in range(cap):
            k = j * cap + c
            index = jnp.where(lane == k, rows[j, c], index)
            index = jnp.where(lane == slots + k, cols[j, c], index)
        index = jnp.where(lane == 2 * slots + j, counts[j], index)
    index = index.astype(F32).astype(BF16)
    for x in range(reps):
        outs[x][:part] = turned[other("rep", x)]
        outs[x][part:] = index


def order_chunks(reps, part, *refs):
    copies = reps // 2 - 1
    chunks, unread, sources = refs[:reps], refs[reps], refs[reps + 1 : reps + 1 + copies]
    mine, index = refs[reps + copies + 1 : reps + copies + 3]
    for source, target in zip(sources, refs[reps + copies + 3 :]):
        target[...] = source[...]
    for x in range(reps):
        mine[other("rep", x)] = chunks[x][:part]
        index[x] = chunks[x][part:].astype(F32).astype(jnp.int32)[:1]


def join(half, *refs):
    out, pairs = refs[-2:]
    for k, ref in enumerate(refs[:half]):
        out[(half - k) % half] = ref[...]
    for k in range(pairs.shape[0]):
        pairs[k] = refs[half + k][...]


def slot_of(index, lists, cap, t, j, c):
    k = j * cap + c
    slots = lists * cap
    return index[t, 0, k], index[t, 0, slots + k], c < index[t, 0, 2 * slots + j]


def relative(groups, lists, x, j):
    mine = lax.axis_index("blk")
    offset = other("rep", x) * lists + j
    return lax.div(lax.bitwise_xor(mine, lax.rem(mine + groups - offset, groups)), 2)


def aggregate(reps, groups, lists, cap, parity, index, *refs):
    blocks, held, start, out = refs[:reps], refs[reps], refs[reps + 1 : -2], refs[-2]
    total = refs[-1]
    total[...] = start[0][...] if start else jnp.zeros_like(total)
    for x in range(reps):
        for j in range(parity, lists, 2):
            place = relative(groups, lists, x, j)
            for c in range(cap):
                row, col, live = slot_of(index, lists, cap, x, j, c)
                product = dot(held[place, col], blocks[x][j * cap + c], 1, 1)
                total[row] += jnp.where(live, product, 0.0)
    out[...] = total[...].astype(out.dtype)


def dense_layer(reps, *refs):
    chunks = refs[:reps]
    cotangents = refs[reps : reps + 2]
    weight, out, dagg, terms, agg, cot, outs = refs[reps + 2 :]
    nodes, width = out.shape
    for x in range(reps):
        origin = other("rep", x)
        cot[origin] = cotangents[x % 2][x // 2]
        for b in range(reps):
            agg[b, origin] = chunks[x][b]
    gw = jnp.zeros((width, width), F32)
    for b in range(reps):
        turned = agg[b].reshape(width, nodes)
        pre = dot(turned, weight[...], 0, 0)
        sigma = jax.nn.sigmoid(pre)
        outs[b] = (pre * sigma).astype(BF16)
        slope = sigma * (1.0 + pre * (1.0 - sigma))
        dpre = (cot[b].astype(F32) * slope).astype(BF16)
        dagg[b] = dot(dpre, weight[...], 1, 1).astype(BF16)
        gw += dot(turned, dpre, 1, 0)
    out[...] = outs[lax.axis_index("rep")]
    terms[...] = gw.astype(BF16).reshape(terms.shape)


def feature_grads(reps, groups, lists, cap, parity, index, *refs):
    blocks, dagg, rest = refs[:reps], refs[reps], refs[reps + 1 :]
    me = lax.axis_index("rep")
    half = groups // 2
    total = rest[-1]
    total[...] = jnp.zeros_like(total)
    for x in range(reps):
        for j in range(parity, lists, 2):
            place = relative(groups, lists, x, j)
            for c in range(cap):
                row, col, live = slot_of(index, lists, cap, x, j, c)

                @pl.when(jnp.logical_and(live, col == me))
                def _():
                    total[place] += dot(blocks[x][j * cap + c], dagg[row], 0, 0)

    if parity:
        terms, send = rest[:2]
        send[:half] = total[...].astype(BF16)
        core = lax.rem(lax.axis_index("blk"), 2)
        send[half:] = terms[1 - core].reshape(-1, *send.shape[1:])


def add_core(half, keep, terms, arrived, own, own_terms, *sends):
    nodes = own.shape[0]
    own[...] = keep[0] + arrived[0].astype(F32)
    core = lax.rem(lax.axis_index("blk"), 2)
    mine = terms[core].astype(F32)
    gw = (mine + arrived[half:].reshape(mine.shape).astype(F32)).astype(BF16)
    own_terms[...] = gw
    for k in range(1, half):
        sends[half - 1 - k][:nodes] = (keep[k] + arrived[k].astype(F32)).astype(BF16)
        sends[half - 1 - k][nodes:] = gw


def add_chips(half, own, own_terms, *refs):
    parts, grads, terms, held = refs[: half - 1], refs[-3], refs[-2], refs[-1]
    nodes = own.shape[0]
    chip = lax.div(lax.axis_index("blk"), 2)
    total = own[...]
    held[chip] = own_terms[...].astype(F32)
    for k in range(1, half):
        total += parts[half - 1 - k][:nodes].astype(F32)
        held[lax.bitwise_xor(chip, k)] = parts[half - 1 - k][nodes:].astype(F32)
    grads[...] = total
    gw = held[0]
    for k in range(1, half):
        gw += held[k]
    terms[...] = gw


def store(grads, rows, grad_feats, out_rows):
    grad_feats[...] = grads[...]
    out_rows[...] = rows[...]


def join_cores(mine, arrived, out):
    core = lax.rem(lax.axis_index("blk"), 2)
    rows = mine.shape[0]
    out[pl.ds(pl.multiple_of(core * rows, rows), rows), :] = mine[...]
    out[pl.ds(pl.multiple_of((1 - core) * rows, rows), rows), :] = arrived[...]


def per_device(feats, weight, cotangent, block_vals, block_rows, block_cols, step_counts):
    reps = lax.axis_size("rep")
    groups = lax.axis_size("blk")
    lists, cap, block = block_vals.shape[2:5]
    nodes, width = feats.shape
    part = width // reps
    slots = lists * cap
    half = groups // 2
    like = jax.ShapeDtypeStruct

    def direct(arrays):
        return [arrays[0]] + [swap(arrays[x], "rep", x) for x in range(1, reps)]

    adjacency = block_vals.reshape(slots, block, block)
    odds = [swap(adjacency, "rep", 1)]
    evens = spread(adjacency, 2)
    chunks = call(
        functools.partial(split_features, reps, lists, cap),
        [like((part + PAD, nodes), BF16)] * reps,
        [VMEM, SMEM, SMEM, SMEM],
        [pltpu.VMEM((reps, part, nodes), BF16)],
        moved=4 * nodes * width,
    )(feats, block_rows[0, 0], block_cols[0, 0], step_counts[0, 0])
    mine, index, *relayed = call(
        functools.partial(order_chunks, reps, part),
        [like((reps, part, nodes), BF16), like((reps, 1, nodes), jnp.int32)]
        + [like((slots, block, block), BF16)] * (reps // 2 - 1),
        [VMEM] * reps + [pl.BlockSpec(memory_space=pl.ANY)] + [VMEM] * (reps // 2 - 1),
        moved=4 * nodes * width,
    )(*direct(chunks), odds[0], *evens[1:])
    odds += [swap(array, "rep", 1) for array in relayed]
    blocks = [array for pair in zip(evens, odds) for array in pair]

    near, cotangents = call(
        functools.partial(join, half),
        [like((half, reps, part, nodes), BF16), like((reps // 2, nodes, width), BF16)],
        [VMEM] * (half + reps // 2) + [pl.BlockSpec(memory_space=pl.ANY)] * (reps // 2 - 1),
        moved=4 * half * nodes * width,
    )(
        mine,
        *[swap(mine, "blk", 2 * k) for k in range(half - 1, 0, -1)],
        *spread(cotangent, 2),
        *odds[1:],
    )
    far = swap(near, "blk", 1)
    slot_flops = 2 * groups * cap * part * block * block
    slot_bytes = 2 * (groups * cap * block * block + groups * nodes * width)

    agg = call(
        functools.partial(aggregate, reps, groups, lists, cap, 0),
        like((reps, part, nodes), F32),
        [SMEM] + [VMEM] * (reps + 1),
        [pltpu.VMEM((reps, part, nodes), F32)],
        flops=slot_flops // 2,
        moved=slot_bytes // 2,
    )(index, *blocks, near)
    agg = call(
        functools.partial(aggregate, reps, groups, lists, cap, 1),
        like((reps, part, nodes), BF16),
        [SMEM] + [VMEM] * (reps + 2),
        [pltpu.VMEM((reps, part, nodes), F32)],
        flops=slot_flops // 2,
        moved=slot_bytes // 2,
    )(index, *blocks, far, agg)

    out_rows, dagg, terms = call(
        functools.partial(dense_layer, reps),
        [
            like((nodes, width), BF16),
            like((reps, nodes, width), BF16),
            like((2, width // 2, width), BF16),
        ],
        [VMEM] * (reps + 3),
        [
            pltpu.VMEM((reps, reps, part, nodes), BF16),
            pltpu.VMEM((reps, nodes, width), BF16),
            pltpu.VMEM((reps, nodes, width), BF16),
        ],
        flops=6 * reps * nodes * width * width,
        moved=2 * reps * 5 * nodes * width,
    )(*direct([agg] * reps), cotangents, swap(cotangents, "rep", 1), weight)

    send = call(
        functools.partial(feature_grads, reps, groups, lists, cap, 1),
        like((half + width // 2 // nodes, nodes, width), BF16),
        [SMEM] + [VMEM] * (reps + 2),
        [pltpu.VMEM((half, nodes, width), F32)],
        flops=slot_flops // 2,
        moved=slot_bytes // 2,
    )(index, *blocks, dagg, terms)
    keep = call(
        functools.partial(feature_grads, reps, groups, lists, cap, 0),
        like((half, nodes, width), F32),
        [SMEM] + [VMEM] * (reps + 1),
        flops=slot_flops // 2,
        moved=slot_bytes // 2,
    )(index, *blocks, dagg)
    own, own_terms, *sends = call(
        functools.partial(add_core, half),
        [like((nodes, width), F32), like((width // 2, width), BF16)]
        + [like((nodes + width // 2, width), BF16)] * (half - 1),
        [VMEM] * 3,
        moved=10 * half * nodes * width,
    )(keep, terms, swap(send, "blk", 1))
    grads, terms = call(
        functools.partial(add_chips, half),
        [like((nodes, width), F32), like((width // 2, width), F32)],
        [VMEM] * (half + 1),
        [pltpu.VMEM((half, width // 2, width), F32)],
        moved=8 * half * nodes * width,
    )(own, own_terms, *[swap(sends[half - 1 - k], "blk", 2 * k) for k in range(half - 1, 0, -1)])
    grad_feats, out_rows = call(
        store,
        [like((nodes, width), F32), like((nodes, width), BF16)],
        [VMEM] * 2,
        moved=12 * nodes * width,
    )(grads, out_rows)
    grad_weight = call(
        join_cores, like((width, width), F32), [VMEM] * 2, moved=8 * width * width
    )(terms, swap(terms, "blk", 1))
    return (out_rows, grad_weight, grad_feats)


def solution(mesh):
    return jax.shard_map(
        per_device,
        mesh=mesh,
        in_specs=(
            P(("blk", "rep"), None),
            P(),
            P(("blk", "rep"), None),
            P("blk", "rep", None, None, None, None),
            P("blk", "rep", None, None),
            P("blk", "rep", None, None),
            P("blk", "rep", None),
        ),
        out_specs=(P(("blk", "rep"), None), P(), P(("blk", "rep"), None)),
        check_vma=False,
    )
```
